128 devices in a mesh: ctx: 16 (over z_hi, x, core), exp: 8 (over y, z_lo).
Axes of the slice: x: 4, y: 4, z: 4 (z_hi: 2, z_lo: 2; z = z_hi * 2 + z_lo), core: 2. Of those that a mesh axis runs over, the one named last changes fastest.
Arguments:
- queries: bfloat16 [6144, 4096], P('ctx', 'exp'), may hold values from -24 to 24
- keys: bfloat16 [6144, 256], P('ctx'), may hold values from -12 to 12
- values: bfloat16 [6144, 256], P('ctx'), may hold values from -6 to 6
- out_grad: bfloat16 [6144, 4096], P('ctx', 'exp'), may hold values from -6 to 6
- moe_grad: bfloat16 [16384, 4096], P(('ctx', 'exp')), may hold values from -4 to 4
- expert_ids: int32 [16384, 8], P(('ctx', 'exp')), may hold values from 0 to 127, as said below
- gate_weights: bfloat16 [16384, 8], P(('ctx', 'exp')), may hold values from 0.19921875 to 1
- saved_gate: bfloat16 [16384, 1536], P(('ctx', 'exp')), may hold values from -6 to 6
- saved_up: bfloat16 [16384, 1536], P(('ctx', 'exp')), may hold values from -6 to 6
- down_weight: bfloat16 [8, 1536, 4096], P('exp'), may hold values from -0.15625 to 0.15625
Outputs:
- query_grad: bfloat16 [6144, 4096], P('ctx', 'exp')
- key_grad: bfloat16 [6144, 256], P(('ctx', 'exp'))
- value_grad: bfloat16 [6144, 256], P(('ctx', 'exp'))
- gate_grad: float32 [16384, 8], P(('ctx', 'exp'))
- gate_pre_grad: bfloat16 [16384, 1536], P(('ctx', 'exp'))
- up_pre_grad: bfloat16 [16384, 1536], P(('ctx', 'exp'))
The draws below stay inside these ranges and needn't reach their ends.
Inputs may be any that keep to these rules, and one draw needn't show every extreme that they name: `expert_ids`: each row names 8 different experts. In each aligned block of 128 rows (the rows of one device) no expert is named by more than 16 rows, and some expert below 8 is named by exactly 16 rows; in the blocks c * 8 to c * 8 + 7 that is the same expert.
All inputs are finite; a program needn't handle non-finite values.
Results may differ from the reference program's by a relative error of at most 0.0052.
Values may be sent and summed in bfloat16 or wider, within the bound.
A program may use at most 128 MiB of HBM per device.

```python
import jax
import jax.numpy as jnp
from jax import lax

D = 4096
FF = 1536
QHEADS = 32
KVHEADS = 2
HEAD = 128
EXPERTS = 128
TOPK = 8
TOK_DEV = 128
LENGTH = 6144
MOE_ROWS = 16384
CAP = 16
FLIGHT = 8
SLOTS = 16384
N_CTX = 16
N_EXP = 8


def key_base(key, low, high):
    base = jax.random.normal(key, (LENGTH, KVHEADS * HEAD), jnp.float32)
    spread = jax.random.uniform(jax.random.fold_in(key, 5), (LENGTH, 1), jnp.float32, low, high)
    return jnp.clip(spread * base, -12.0, 12.0)


def draw_keys(key, part):
    shared = key_base(key, 1.0, 1.0)
    return shared.astype(jnp.bfloat16)


def draw_queries(key, part):
    key = jax.random.fold_in(key, 12)
    own_draw = jnp.clip(jax.random.normal(key, (LENGTH, QHEADS * HEAD), jnp.float32), -6.0, 6.0)
    return own_draw.astype(jnp.bfloat16)


def draw_expert_ids(key, part):
    key = jax.random.fold_in(key, 21)
    mean_load = TOK_DEV * TOPK // EXPERTS

    def one_block(block_number):
        block_key = jax.random.fold_in(key, block_number)
        order = jax.random.permutation(jax.random.fold_in(block_key, 1), EXPERTS).astype(jnp.int32)
        shifts = jax.random.randint(jax.random.fold_in(block_key, 2), (EXPERTS // 2,), -mean_load, mean_load + 1, jnp.int32)
        full_expert = jax.random.randint(jax.random.fold_in(key, 100000 + block_number // FLIGHT), (), 0, FLIGHT, jnp.int32)
        place = jnp.argmax(order == full_expert).astype(jnp.int32)
        forced = jnp.where(place % 2 == 0, mean_load, -mean_load).astype(jnp.int32)
        shifts = jnp.where(jnp.arange(EXPERTS // 2, dtype=jnp.int32) == place // 2, forced, shifts)
        loads = jnp.stack([mean_load + shifts, mean_load - shifts], axis=1).reshape(-1)
        ends = jnp.cumsum(loads).astype(jnp.int32)
        position = jnp.arange(TOK_DEV * TOPK, dtype=jnp.int32)
        which = jnp.searchsorted(ends, position, side='right')
        chosen = order[which]
        table = chosen.reshape(TOPK, TOK_DEV).T
        row_order = jax.random.permutation(jax.random.fold_in(block_key, 3), TOK_DEV)
        return table[row_order]
    blocks_out = jax.vmap(one_block)(jnp.arange(MOE_ROWS // TOK_DEV, dtype=jnp.int32))
    return blocks_out.reshape(MOE_ROWS, TOPK).astype(jnp.int32)


def steps_of(stream_key, extent, cuts, smallest, high):
    level = 1.0
    for dim, parts in cuts:
        steps = jax.random.uniform(jax.random.fold_in(jax.random.fold_in(stream_key, 6), dim), (parts,), jnp.float32, smallest / len(cuts), high / len(cuts))
        level = level * jnp.repeat(jnp.exp(steps), extent[dim] // parts).reshape((-1,) + (1,) * (len(extent) - 1 - dim))
    return level


def normal_values(stream_key, dims, scale, bound, cuts=(), kind=jnp.bfloat16):
    result = jax.random.normal(stream_key, dims, jnp.float32) * scale
    if len(cuts) > 0:
        result = steps_of(stream_key, dims, cuts, -0.22, 0.18) * result
    return jnp.clip(result, min=-bound, max=bound).astype(kind)


def setup_inputs(seed: int = 0) -> dict:
    seeds = jax.random.split(jax.random.key(seed), 11)
    return {
        "queries": draw_queries(jax.random.fold_in(seeds[10], 71), 0),
        "keys": draw_keys(jax.random.fold_in(seeds[10], 71), 0),
        "values": normal_values(seeds[2], (LENGTH, KVHEADS * HEAD), 1.0, 6.0, ((0, 16),)),
        "out_grad": normal_values(seeds[3], (LENGTH, QHEADS * HEAD), 1.0, 6.0, ((0, 16), (1, 8))),
        "moe_grad": normal_values(seeds[4], (MOE_ROWS, D), 0.5, 4.0, ((0, 128),)),
        "expert_ids": draw_expert_ids(jax.random.fold_in(seeds[10], 71), 0),
        "gate_weights": jnp.clip(0.19921875 + 0.80078125 * jax.random.uniform(seeds[6], (MOE_ROWS, TOPK), jnp.float32) ** steps_of(seeds[6], (MOE_ROWS, TOPK), ((0, 128),), -0.2, 0.2), 0.19921875, 1.0).astype(jnp.bfloat16),
        "saved_gate": normal_values(seeds[7], (SLOTS, FF), 1.0, 6.0, ((0, 128),)),
        "saved_up": normal_values(seeds[8], (SLOTS, FF), 1.0, 6.0, ((0, 128),)),
        "down_weight": normal_values(seeds[9], (FLIGHT, FF, D), FF ** -0.5, 0.15625, ((0, 8),)),
    }


def head_grads(queries, keys, values, out_grad, head):
    head_group = QHEADS // KVHEADS
    kv_head = head // head_group
    score_scale = HEAD ** -0.5
    query_h = lax.dynamic_slice_in_dim(queries, head * HEAD, HEAD, 1)
    grad_h = lax.dynamic_slice_in_dim(out_grad, head * HEAD, HEAD, 1)
    key_h = lax.dynamic_slice_in_dim(keys, kv_head * HEAD, HEAD, 1)
    value_h = lax.dynamic_slice_in_dim(values, kv_head * HEAD, HEAD, 1)
    scores = jnp.dot(query_h, key_h.T, preferred_element_type=jnp.float32) * score_scale
    positions = jnp.arange(LENGTH, dtype=jnp.int32)
    visible = positions[:, None] >= positions[None, :]
    scores = jnp.where(visible, scores, -jnp.inf)
    log_total = jax.nn.logsumexp(scores, axis=1, keepdims=True)
    probabilities = jnp.exp(scores - log_total)
    prob_grad = jnp.dot(grad_h, value_h.T, preferred_element_type=jnp.float32)
    row_delta = jnp.sum(probabilities * prob_grad, axis=1, keepdims=True)
    score_grad = probabilities * (prob_grad - row_delta)
    probs_b = probabilities.astype(jnp.bfloat16)
    score_b = score_grad.astype(jnp.bfloat16)
    query_grad = jnp.dot(score_b, key_h, preferred_element_type=jnp.float32) * score_scale
    key_grad = jnp.dot(score_b.T, query_h, preferred_element_type=jnp.float32) * score_scale
    value_grad = jnp.dot(probs_b.T, grad_h, preferred_element_type=jnp.float32)
    return query_grad, key_grad, value_grad


def expert_part(moe_grad, expert_ids, gate_weights, saved_gate, saved_up, down_weight):
    blocks = MOE_ROWS // TOK_DEV
    routes = TOK_DEV * TOPK
    route_ids = expert_ids.reshape(blocks, routes)
    computed = jnp.arange(N_EXP, dtype=jnp.int32)
    matches = (route_ids[:, :, None] == computed[None, None, :]).astype(jnp.int32)
    earlier = jnp.cumsum(matches, axis=1) - matches
    slot_rank = jnp.sum(earlier * matches, axis=2)
    in_flight = route_ids < N_EXP
    block_index = jnp.arange(blocks, dtype=jnp.int32)[:, None]
    ctx_index = block_index // N_EXP
    source = block_index % N_EXP
    slot_row = ((ctx_index * N_EXP + route_ids) * N_EXP + source) * CAP + slot_rank
    slot_row = jnp.where(in_flight, slot_row, SLOTS).reshape(-1).astype(jnp.int32)
    token_row = (block_index * TOK_DEV + jnp.arange(routes, dtype=jnp.int32)[None, :] // TOPK).reshape(-1)
    sent = jnp.zeros((SLOTS + 1, D), jnp.bfloat16).at[slot_row].set(moe_grad[token_row])[:SLOTS]
    slot_weight = jnp.zeros((SLOTS + 1,), jnp.bfloat16).at[slot_row].set(gate_weights.reshape(-1))[:SLOTS]
    gate_f = saved_gate.astype(jnp.float32)
    up_f = saved_up.astype(jnp.float32)
    sigmoid_gate = jax.nn.sigmoid(gate_f)
    activation = (gate_f * sigmoid_gate * up_f).astype(jnp.bfloat16)
    weights_f = down_weight.astype(jnp.float32)
    act_blocks = activation.astype(jnp.float32).reshape(N_CTX, N_EXP, N_EXP * CAP, FF)
    expert_out = jnp.einsum("cerf,efd->cerd", act_blocks, weights_f).reshape(SLOTS, D)
    sent_f = sent.astype(jnp.float32)
    slot_score = jnp.sum(sent_f * expert_out, axis=1)
    back_grad = jnp.einsum("cerd,efd->cerf", sent_f.reshape(N_CTX, N_EXP, N_EXP * CAP, D), weights_f).reshape(SLOTS, FF)
    act_grad = slot_weight.astype(jnp.float32)[:, None] * back_grad
    gate_pre_grad = (act_grad * up_f * sigmoid_gate * (1.0 + gate_f * (1.0 - sigmoid_gate))).astype(jnp.bfloat16)
    up_pre_grad = (act_grad * gate_f * sigmoid_gate).astype(jnp.bfloat16)
    padded = jnp.concatenate([slot_score, jnp.zeros((1,), jnp.float32)])
    gate_grad = padded[slot_row].reshape(MOE_ROWS, TOPK)
    return gate_grad, gate_pre_grad, up_pre_grad


def reference(queries, keys, values, out_grad, moe_grad, expert_ids, gate_weights, saved_gate, saved_up, down_weight):
    head_list = jnp.arange(QHEADS, dtype=jnp.int32)
    query_parts, key_parts, value_parts = lax.map(lambda head: head_grads(queries, keys, values, out_grad, head), head_list)
    head_group = QHEADS // KVHEADS
    query_grad = query_parts.transpose(1, 0, 2).reshape(LENGTH, QHEADS * HEAD).astype(jnp.bfloat16)
    key_grad = key_parts.reshape(KVHEADS, head_group, LENGTH, HEAD).sum(axis=1).transpose(1, 0, 2).reshape(LENGTH, KVHEADS * HEAD).astype(jnp.bfloat16)
    value_grad = value_parts.reshape(KVHEADS, head_group, LENGTH, HEAD).sum(axis=1).transpose(1, 0, 2).reshape(LENGTH, KVHEADS * HEAD).astype(jnp.bfloat16)
    gate_grad, gate_pre_grad, up_pre_grad = expert_part(moe_grad, expert_ids, gate_weights, saved_gate, saved_up, down_weight)
    return (query_grad, key_grad, value_grad, gate_grad, gate_pre_grad, up_pre_grad)
```

```python
import functools

import jax
import jax.numpy as jnp
from jax import lax
from jax.experimental import pallas as pl
from jax.experimental.pallas import tpu as pltpu
from jax.sharding import PartitionSpec as P

QHEADS = 32
KVHEADS = 2
HEAD = 128
TOPK = 8
CAP = 16
LOG2E = 1.4426950408889634
SCALE = HEAD ** (-0.5)
MESH = pl.DeviceIdType.MESH
NT = (((1,), (1,)), ((), ()))
TN = (((0,), (0,)), ((), ()))
NN = (((1,), (0,)), ((), ()))


def dot(a, b, dims):
    return lax.dot_general(a, b, dims, preferred_element_type=jnp.float32)


def body(
    q_ref,
    k_ref,
    v_ref,
    do_ref,
    moe_ref,
    ids_ref,
    gw_ref,
    sg_ref,
    su_ref,
    w_ref,
    dq_ref,
    dk_ref,
    dv_ref,
    gg_ref,
    gp_ref,
    up_ref,
    kv,
    qd_own,
    qd_send,
    qd_for,
    probs,
    dprob,
    maxes,
    dq_acc,
    dkv,
    dq_send,
    dq_recv,
    merge_recv,
    ea_recv,
    total,
    eb_recv,
    send_rows,
    recv_rows,
    onehot,
    score_send,
    score_recv,
    w_buf,
    w_sem,
    a_sem,
    b_sem,
    relay_sem,
    c_sem,
    d_sem,
    merge_sem,
    ea_sem,
    eb_sem,
    score_sem,
):
    c = lax.axis_index("ctx")
    e = lax.axis_index("exp")
    rows = q_ref.shape[0]
    sub = rows // 2
    heads = q_ref.shape[1] // HEAD
    width = heads * sub
    tokens, model = moe_ref.shape
    hidden = sg_ref.shape[1]
    slots = sg_ref.shape[0]
    z_hi, x, core = c // 8, (c // 2) % 4, c % 2
    chip = c // 2
    y, z_lo = e // 2, e % 2
    kv_head = e // 4

    def ctx_peer(turn, shift):
        far_z = 1 - z_hi if turn else z_hi
        far_zl = 1 - z_lo if turn else z_lo
        far_chip = far_z * 4 + (x + shift) % 4
        return far_chip, (far_chip * 2 + core, y * 2 + far_zl)

    relations = [(0, 1), (0, 3), (1, 0), (0, 2), (1, 1), (1, 3), (1, 2)]
    other_core = (c + 1 - 2 * core, e)
    partner = (15 - c, y * 2 + 1 - z_lo)

    def remote(src, dst, sems, index, device):
        return pltpu.make_async_remote_copy(
            src_ref=src,
            dst_ref=dst,
            send_sem=sems.at[0, index],
            recv_sem=sems.at[1, index],
            device_id=device,
            device_id_type=MESH,
        )

    chunk = w_buf.shape[1]
    chunks = hidden // chunk

    def weight_copy(i, slot):
        return pltpu.make_async_copy(
            w_ref.at[0, pl.ds(pl.multiple_of(i * chunk, chunk), chunk), :],
            w_buf.at[slot],
            w_sem.at[slot],
        )

    weight_copy(0, 0).start()
    weight_copy(1, 1).start()

    barrier = pltpu.get_barrier_semaphore()
    peers = [ctx_peer(turn, shift)[1] for turn, shift in relations]
    peers += [(c, (e + step) % 8) for step in range(1, 8)]
    peers += [other_core, partner]
    for peer in peers:
        pl.semaphore_signal(barrier, inc=1, device_id=peer, device_id_type=MESH)

    head_cols = pl.ds(pl.multiple_of(kv_head * HEAD, HEAD), HEAD)
    kv[core, chip, :, 0:HEAD] = k_ref[:, head_cols]
    kv[core, chip, :, HEAD : 2 * HEAD] = v_ref[:, head_cols]
    for h in range(heads):
        cols = slice(h * HEAD, (h + 1) * HEAD)
        rows_h = slice(h * sub, (h + 1) * sub)
        qd_own[rows_h, 0:HEAD] = q_ref[0:sub, cols]
        qd_own[rows_h, HEAD : 2 * HEAD] = do_ref[0:sub, cols]
        qd_send[rows_h, 0:HEAD] = q_ref[sub : 2 * sub, cols]
        qd_send[rows_h, HEAD : 2 * HEAD] = do_ref[sub : 2 * sub, cols]

    pl.semaphore_wait(barrier, len(peers))

    own_block = kv.at[core, chip]
    b_copies = []
    for n, (turn, shift) in enumerate(relations):
        copy = remote(own_block, own_block, b_sem, n, ctx_peer(turn, shift)[1])
        copy.start()
        b_copies.append(copy)
    relays = [remote(own_block, own_block, relay_sem, 7, other_core)]
    relays[0].start()
    c_copy = remote(qd_send, qd_for, c_sem, 0, partner)
    c_copy.start()

    lane = lax.broadcasted_iota(jnp.int32, (tokens, slots), 1)
    slot_expert = lane // CAP
    ids = ids_ref[...]
    weights = gw_ref[...].astype(jnp.float32)
    match = jnp.zeros((tokens, slots), jnp.float32)
    weight_of = jnp.zeros((tokens, slots), jnp.float32)
    for k in range(TOPK):
        hit = ids[:, k : k + 1] == slot_expert
        match = jnp.where(hit, 1.0, match)
        weight_of = jnp.where(hit, weights[:, k : k + 1], weight_of)
    row = lax.broadcasted_iota(jnp.int32, (tokens, tokens), 0)
    col = lax.broadcasted_iota(jnp.int32, (tokens, tokens), 1)
    lower = jnp.where(col < row, 1.0, 0.0).astype(jnp.bfloat16)
    rank = dot(lower, match.astype(jnp.bfloat16), NN)
    place = jnp.where(rank == (lane % CAP).astype(jnp.float32), match, 0.0)
    onehot[...] = place
    place_b = place.astype(jnp.bfloat16)
    step_cols = 512

    def gather_cols(i, carry):
        cols = pl.ds(pl.multiple_of(i * step_cols, step_cols), step_cols)
        send_rows[:, cols] = dot(place_b, moe_ref[:, cols], TN).astype(jnp.bfloat16)
        return carry

    lax.fori_loop(0, model // step_cols, gather_cols, 0)
    slot_weight = dot(
        (place * weight_of).astype(jnp.bfloat16), jnp.ones((tokens, HEAD), jnp.bfloat16), TN
    )
    send_rows[:, model : model + HEAD] = slot_weight.astype(jnp.bfloat16)
    own_rows = pl.ds(pl.multiple_of(e * CAP, CAP), CAP)
    a_copies = []
    for step in range(1, 8):
        far = (e + step) % 8
        copy = remote(
            send_rows.at[pl.ds(pl.multiple_of(far * CAP, CAP), CAP), :],
            recv_rows.at[own_rows, :],
            a_sem,
            step - 1,
            (c, far),
        )
        copy.start()
        a_copies.append(copy)
    recv_rows[own_rows, :] = send_rows[own_rows, :]

    dkv[...] = jnp.zeros_like(dkv)

    for n, (turn, shift) in enumerate(relations):
        b_copies[n].wait()
        from_chip = ctx_peer(turn, 4 - shift)[0]
        block = kv.at[core, from_chip]
        relay = remote(block, block, relay_sem, n, other_core)
        relay.start()
        relays.append(relay)
    for relay in relays:
        relay.wait()

    def attend(qd, sub_index, base):
        last = sub_index // 2
        q = qd[:, 0:HEAD]
        do = qd[:, HEAD : 2 * HEAD]

        def first(j, stats, masked):
            m, l, d = stats
            s = dot(kv[j % 2, j // 2, :, 0:HEAD], q, NT) * (SCALE * LOG2E)
            dp = dot(kv[j % 2, j // 2, :, HEAD : 2 * HEAD], do, NT)
            if masked:
                key_at = lax.broadcasted_iota(jnp.int32, (rows, width), 0) + j * rows
                query_at = (
                    lax.broadcasted_iota(jnp.int32, (rows, width), 1) % sub + sub_index * sub
                )
                s = jnp.where(key_at <= query_at, s, -jnp.inf)
            new = jnp.maximum(m, jnp.max(s, axis=0, keepdims=True))
            factor = jnp.exp2(m - new)
            ex = jnp.exp2(s - new)
            l = l * factor + jnp.sum(ex, axis=0, keepdims=True)
            d = d * factor + jnp.sum(ex * dp, axis=0, keepdims=True)
            probs[base + j] = ex.astype(probs.dtype)
            dprob[base + j] = dp
            maxes[base + j] = jnp.broadcast_to(new, (8, width))
            return (new, l, d)

        zero = jnp.zeros((1, width), jnp.float32)
        stats = lax.fori_loop(
            0, last, lambda j, s: first(j, s, False), (jnp.full((1, width), -1e30), zero, zero)
        )
        m, l, d = first(last, stats, True)
        inverse = 1.0 / l
        delta = d * inverse
        dq_acc[...] = jnp.zeros_like(dq_acc)

        def second(j, carry):
            scale = jnp.exp2(maxes[base + j][0:1] - m) * inverse
            p = probs[base + j].astype(jnp.float32) * scale
            ds = p * (dprob[base + j] - delta)
            p_b = p.astype(jnp.bfloat16)
            ds_b = ds.astype(jnp.bfloat16)
            dkv[j % 2, j // 2, :, 0:HEAD] += dot(ds_b, q, NN)
            dkv[j % 2, j // 2, :, HEAD : 2 * HEAD] += dot(p_b, do, NN)
            dq_acc[...] += dot(kv[j % 2, j // 2, :, 0:HEAD], ds_b, TN)
            return carry

        lax.fori_loop(0, last + 1, second, 0)
        return (dq_acc[...] * SCALE).T.astype(jnp.bfloat16)

    dq_own = attend(qd_own, 2 * c, 0)
    for h in range(heads):
        dq_ref[0:sub, h * HEAD : (h + 1) * HEAD] = dq_own[h * sub : (h + 1) * sub]
    c_copy.wait()
    dq_send[...] = attend(qd_for, 31 - 2 * c, 0)
    d_copy = remote(dq_send, dq_recv, d_sem, 0, partner)
    d_copy.start()

    far_core = 1 - core
    kv[far_core] = dkv[far_core].astype(jnp.bfloat16)
    merge_copy = remote(kv.at[far_core], merge_recv, merge_sem, 0, other_core)
    merge_copy.start()
    merge_copy.wait()
    ea_copies = []
    for n, (turn, shift) in enumerate(relations):
        far_chip, device = ctx_peer(turn, shift)
        kv[core, far_chip] = (
            dkv[core, far_chip] + merge_recv[far_chip].astype(jnp.float32)
        ).astype(jnp.bfloat16)
        copy = remote(kv.at[core, far_chip], ea_recv.at[n], ea_sem, n, device)
        copy.start()
        ea_copies.append(copy)
    total[...] = dkv[core, chip] + merge_recv[chip].astype(jnp.float32)

    for copy in a_copies:
        copy.wait()
    weight_col = recv_rows[:, model : model + HEAD].astype(jnp.float32)
    weight_wide = jnp.concatenate([weight_col] * (chunk // HEAD), axis=1)

    def expert_step(i, score):
        slot = i % 2
        weight_copy(i, slot).wait()
        cols = pl.ds(pl.multiple_of(i * chunk, chunk), chunk)
        back = dot(recv_rows[:, 0:model], w_buf[slot], NT)

        @pl.when(i + 2 < chunks)
        def _():
            weight_copy(i + 2, slot).start()

        g = sg_ref[:, cols].astype(jnp.float32)
        u = su_ref[:, cols].astype(jnp.float32)
        sig = 1.0 / (1.0 + jnp.exp(-g))
        silu = g * sig
        act = (silu * u).astype(jnp.bfloat16).astype(jnp.float32)
        act_grad = weight_wide * back
        gp_ref[:, cols] = (act_grad * u * sig * (1.0 + g * (1.0 - sig))).astype(jnp.bfloat16)
        up_ref[:, cols] = (act_grad * silu).astype(jnp.bfloat16)
        return score + jnp.sum(act * back, axis=1, keepdims=True)

    score = lax.fori_loop(0, chunks, expert_step, jnp.zeros((slots, 1), jnp.float32))
    score_send[...] = jnp.broadcast_to(score, (slots, HEAD))
    score_copies = []
    for step in range(1, 8):
        far = (e + step) % 8
        copy = remote(
            score_send.at[pl.ds(pl.multiple_of(far * CAP, CAP), CAP), :],
            score_recv.at[own_rows, :],
            score_sem,
            step - 1,
            (c, far),
        )
        copy.start()
        score_copies.append(copy)
    score_recv[own_rows, :] = score_send[own_rows, :]

    for n in range(7):
        ea_copies[n].wait()
        total[...] += ea_recv[n].astype(jnp.float32)
    part = rows // 8
    eb_copies = []
    for step in range(1, 8):
        far = (e + step) % 8
        copy = remote(
            total.at[pl.ds(pl.multiple_of(far * part, part), part), :],
            eb_recv.at[e],
            eb_sem,
            step - 1,
            (c, far),
        )
        copy.start()
        eb_copies.append(copy)
    eb_recv[e] = total[pl.ds(pl.multiple_of(e * part, part), part), :]

    for copy in score_copies:
        copy.wait()
    score_row = score_recv[...].T[0:1, :]
    picked = onehot[...] * score_row
    out_lane = lax.broadcasted_iota(jnp.int32, (tokens, TOPK), 1)
    gate = jnp.zeros((tokens, TOPK), jnp.float32)
    for k in range(TOPK):
        value = jnp.sum(
            jnp.where(ids[:, k : k + 1] == slot_expert, picked, 0.0), axis=1, keepdims=True
        )
        gate = jnp.where(out_lane == k, value, gate)
    gg_ref[...] = gate

    d_copy.wait()
    for h in range(heads):
        dq_ref[sub : 2 * sub, h * HEAD : (h + 1) * HEAD] = dq_recv[h * sub : (h + 1) * sub]

    for copy in eb_copies:
        copy.wait()
    for kv_index in range(KVHEADS):
        sums = eb_recv[4 * kv_index]
        for n in range(1, 4):
            sums = sums + eb_recv[4 * kv_index + n]
        cols = slice(kv_index * HEAD, (kv_index + 1) * HEAD)
        dk_ref[:, cols] = (sums[:, 0:HEAD] * SCALE).astype(jnp.bfloat16)
        dv_ref[:, cols] = sums[:, HEAD : 2 * HEAD].astype(jnp.bfloat16)


def shards(*arrays):
    queries, keys, _, _, moe_grad, expert_ids, _, saved_gate, _, _ = arrays
    rows, columns = queries.shape
    sub = rows // 2
    width = columns // HEAD * sub
    tokens, model = moe_grad.shape
    slots, hidden = saved_gate.shape
    bf16, f32 = jnp.bfloat16, jnp.float32
    vmem = pl.BlockSpec(memory_space=pltpu.VMEM)
    dma = pltpu.SemaphoreType.DMA
    return pl.pallas_call(
        body,
        out_shape=(
            jax.ShapeDtypeStruct((rows, columns), bf16),
            jax.ShapeDtypeStruct((rows // 8, 2 * HEAD), bf16),
            jax.ShapeDtypeStruct((rows // 8, 2 * HEAD), bf16),
            jax.ShapeDtypeStruct((tokens, TOPK), f32),
            jax.ShapeDtypeStruct((slots, hidden), bf16),
            jax.ShapeDtypeStruct((slots, hidden), bf16),
        ),
        in_specs=[vmem] * 9 + [pl.BlockSpec(memory_space=pl.ANY)],
        out_specs=(vmem,) * 6,
        scratch_shapes=[
            pltpu.VMEM((2, 8, rows, 2 * HEAD), bf16),
            pltpu.VMEM((width, 2 * HEAD), bf16),
            pltpu.VMEM((width, 2 * HEAD), bf16),
            pltpu.VMEM((width, 2 * HEAD), bf16),
            pltpu.VMEM((16, rows, width), bf16),
            pltpu.VMEM((16, rows, width), f32),
            pltpu.VMEM((16, 8, width), f32),
            pltpu.VMEM((HEAD, width), f32),
            pltpu.VMEM((2, 8, rows, 2 * HEAD), f32),
            pltpu.VMEM((width, HEAD), bf16),
            pltpu.VMEM((width, HEAD), bf16),
            pltpu.VMEM((8, rows, 2 * HEAD), bf16),
            pltpu.VMEM((7, rows, 2 * HEAD), bf16),
            pltpu.VMEM((rows, 2 * HEAD), f32),
            pltpu.VMEM((8, rows // 8, 2 * HEAD), f32),
            pltpu.VMEM((slots, model + HEAD), bf16),
            pltpu.VMEM((slots, model + HEAD), bf16),
            pltpu.VMEM((tokens, slots), f32),
            pltpu.VMEM((slots, HEAD), f32),
            pltpu.VMEM((slots, HEAD), f32),
            pltpu.VMEM((2, 256, model), bf16),
            dma((2,)),
            dma((2, 7)),
            dma((2, 7)),
            dma((2, 8)),
            dma((2, 1)),
            dma((2, 1)),
            dma((2, 1)),
            dma((2, 7)),
            dma((2, 7)),
            dma((2, 7)),
        ],
        compiler_params=pltpu.CompilerParams(
            collective_id=0, has_side_effects=True, vmem_limit_bytes=60 * 1024 * 1024
        ),
    )(*arrays)


def solution(mesh):
    both = ("ctx", "exp")
    in_specs = (
        P("ctx", "exp"),
        P("ctx", None),
        P("ctx", None),
        P("ctx", "exp"),
        P(both, None),
        P(both, None),
        P(both, None),
        P(both, None),
        P(both, None),
        P("exp", None, None),
    )
    out_specs = (
        P("ctx", "exp"),
        P(both, None),
        P(both, None),
        P(both, None),
        P(both, None),
        P(both, None),
    )
    return jax.shard_map(shards, mesh=mesh, in_specs=in_specs, out_specs=out_specs, check_vma=False)
```

```python
import jax
import jax.numpy as jnp
from jax import lax
from jax.experimental import pallas as pl
from jax.experimental.pallas import tpu as pltpu
from jax.sharding import PartitionSpec as P

KVHEADS = 2
HEAD = 128
TOPK = 8
CAP = 16
LOG2E = 1.4426950408889634
SCALE = HEAD ** (-0.5)
MESH = pl.DeviceIdType.MESH
NT = (((1,), (1,)), ((), ()))
TN = (((0,), (0,)), ((), ()))
NN = (((1,), (0,)), ((), ()))


def dot(a, b, dims):
    return lax.dot_general(a, b, dims, preferred_element_type=jnp.float32)


def flip(a, b):
    return a + b - 2 * a * b


def body(
    q_ref,
    k_ref,
    v_ref,
    do_ref,
    moe_ref,
    ids_ref,
    gw_ref,
    sg_ref,
    su_ref,
    w_ref,
    dq_ref,
    dk_ref,
    dv_ref,
    gg_ref,
    gp_ref,
    up_ref,
    kv,
    qd,
    qd_send,
    probs,
    dprob,
    maxes,
    stats,
    dq_acc,
    dkv,
    dqs,
    dq_recv,
    merge_recv,
    e1_recv,
    e2_send,
    e2_recv,
    total,
    ebk,
    ebv,
    moe,
    send_rows,
    recv_rows,
    onehot,
    score_send,
    score_recv,
    sg,
    su,
    gp,
    up,
    dk_out,
    dv_out,
    gg_out,
    w_buf,
    w_sem,
    in_sem,
    out_sem,
    a_sem,
    s1_sem,
    s2_sem,
    relay_sem,
    c_sem,
    d_sem,
    merge_sem,
    e1_sem,
    e2_sem,
    ebk_sem,
    ebv_sem,
    score_sem,
):
    c = lax.axis_index("ctx")
    e = lax.axis_index("exp")
    rows = k_ref.shape[0]
    sub = rows // 2
    heads = q_ref.shape[1] // HEAD
    width = heads * sub
    tokens, model = moe_ref.shape
    slots, hidden = sg_ref.shape
    z_hi, x, core = c // 8, (c // 2) % 4, c % 2
    chip = c // 2
    y, z_lo = e // 2, e % 2
    y_half = y % 2
    kv_head = e // 4

    def far_z(t):
        return t // 4

    def shift(t):
        m = t % 4
        return m + m // 2 - 2 * (m // 3)

    def from_chip(t):
        return flip(z_hi, far_z(t)) * 4 + (x + 4 - shift(t)) % 4

    def to_chip(t):
        return flip(z_hi, far_z(t)) * 4 + (x + shift(t)) % 4

    def to_device(t):
        return (to_chip(t) * 2 + core, y * 2 + flip(z_lo, far_z(t)))

    other_core = (c + 1 - 2 * core, e)
    partner = (15 - c, y * 2 + 1 - z_lo)
    z_mate = (c, y * 2 + 1 - z_lo)
    y_mate = (c, (y + 1 - 2 * y_half) * 2 + z_lo)

    def remote(src, dst, send_sem, recv_sem, device):
        return pltpu.make_async_remote_copy(
            src_ref=src,
            dst_ref=dst,
            send_sem=send_sem,
            recv_sem=recv_sem,
            device_id=device,
            device_id_type=MESH,
        )

    def half(index):
        return pl.ds(pl.multiple_of(index * sub, sub), sub)

    barrier = pltpu.get_barrier_semaphore()
    peers = [to_device(t) for t in range(1, 8)]
    peers += [(c, (e + step) % 8) for step in range(1, 8)]
    peers += [other_core, partner]
    for peer in peers:
        pl.semaphore_signal(barrier, inc=1, device_id=peer, device_id_type=MESH)

    head_cols = pl.ds(pl.multiple_of(kv_head * HEAD, HEAD), HEAD)
    pairs = [
        (k_ref.at[:, head_cols], kv.at[core, chip, 0]),
        (v_ref.at[:, head_cols], kv.at[core, chip, 1]),
    ]
    for n, ref in enumerate((q_ref, do_ref)):
        for h in range(heads):
            cols = pl.ds(h * HEAD, HEAD)
            pairs.append((ref.at[pl.ds(sub, sub), cols], qd_send.at[n, pl.ds(h * sub, sub), :]))
    for n, ref in enumerate((q_ref, do_ref)):
        for h in range(heads):
            cols = pl.ds(h * HEAD, HEAD)
            pairs.append((ref.at[pl.ds(0, sub), cols], qd.at[0, n, pl.ds(h * sub, sub), :]))
    pairs += [(moe_ref, moe), (sg_ref, sg), (su_ref, su)]
    loads = [
        pltpu.make_async_copy(src, dst, in_sem.at[n]) for n, (src, dst) in enumerate(pairs)
    ]
    for load in loads[: 2 + 2 * heads]:
        load.start()

    chunk = w_buf.shape[1]
    chunks = hidden // chunk

    def weight_copy(i, slot):
        return pltpu.make_async_copy(
            w_ref.at[0, pl.ds(pl.multiple_of(i * chunk, chunk), chunk), :],
            w_buf.at[slot],
            w_sem.at[slot],
        )

    for load in loads[: 2 + 2 * heads]:
        load.wait()
    pl.semaphore_wait(barrier, len(peers))

    c_copy = remote(qd_send, qd.at[1], c_sem.at[0], c_sem.at[1], partner)

    def first_hop(t, n):
        if isinstance(t, int) and t > 4:
            block, index = from_chip(4), 1 - z_lo if n == 0 else y_half
            device = ((chip - x + (x + shift(t)) % 4) * 2 + core, e)
        else:
            block, index = chip, z_lo if n == 0 else y_half
            device = to_device(t)
        piece = kv.at[core, block, n, half(index), :]
        return remote(piece, piece, s1_sem.at[0, t, n], s1_sem.at[1, t, n], device)

    def second_hop(t, n):
        index = flip(z_lo, far_z(t)) if n == 0 else y_half
        piece = kv.at[core, from_chip(t), n, half(index), :]
        mate = z_mate if n == 0 else y_mate
        return remote(piece, piece, s2_sem.at[0, t, n], s2_sem.at[1, t, n], mate)

    def relay(t):
        block = kv.at[core, from_chip(t)]
        return remote(block, block, relay_sem.at[0, t], relay_sem.at[1, t], other_core)

    for n in range(2):
        first_hop(4, n).start()
    c_copy.start()
    for t in range(1, 4):
        for n in range(2):
            first_hop(t, n).start()
    relay(0).start()
    weight_copy(0, 0).start()
    weight_copy(1, 1).start()
    for load in loads[2 + 2 * heads :]:
        load.start()

    slot_row = lax.broadcasted_iota(jnp.int32, (slots, tokens), 0)
    slot_expert = slot_row // CAP
    ids = ids_ref[...]
    weights = gw_ref[...].astype(jnp.float32)
    match = jnp.zeros((slots, tokens), jnp.float32)
    weight_of = jnp.zeros((slots, tokens), jnp.float32)
    for k in range(TOPK):
        hit = ids[k : k + 1, :] == slot_expert
        match = jnp.where(hit, 1.0, match)
        weight_of = jnp.where(hit, weights[k : k + 1, :], weight_of)
    row = lax.broadcasted_iota(jnp.int32, (tokens, tokens), 0)
    col = lax.broadcasted_iota(jnp.int32, (tokens, tokens), 1)
    earlier = jnp.where(row < col, 1.0, 0.0).astype(jnp.bfloat16)
    rank = dot(match.astype(jnp.bfloat16), earlier, NN)
    place = jnp.where(rank == (slot_row % CAP).astype(jnp.float32), match, 0.0)
    onehot[...] = place
    place_b = place.astype(jnp.bfloat16)
    for load in loads[2 + 2 * heads :]:
        load.wait()
    step_cols = 512

    def gather_cols(i, carry):
        cols = pl.ds(pl.multiple_of(i * step_cols, step_cols), step_cols)
        send_rows[:, cols] = dot(place_b, moe[:, cols], NN).astype(jnp.bfloat16)
        return carry

    lax.fori_loop(0, model // step_cols, gather_cols, 0)
    slot_weight = dot(
        (place * weight_of).astype(jnp.bfloat16), jnp.ones((tokens, HEAD), jnp.bfloat16), NN
    )
    send_rows[:, model : model + HEAD] = slot_weight.astype(jnp.bfloat16)
    own_rows = pl.ds(pl.multiple_of(e * CAP, CAP), CAP)

    def far_rows(far):
        return pl.ds(pl.multiple_of(far * CAP, CAP), CAP)

    a_copies = []
    for step in range(1, 8):
        far = (e + step) % 8
        copy = remote(
            send_rows.at[far_rows(far), :],
            recv_rows.at[own_rows, :],
            a_sem.at[0, step - 1],
            a_sem.at[1, step - 1],
            (c, far),
        )
        copy.start()
        a_copies.append(copy)
    recv_rows[own_rows, :] = send_rows[own_rows, :]

    dkv[...] = jnp.zeros_like(dkv)
    dq_acc[...] = jnp.zeros_like(dq_acc)
    for s in range(2):
        stats[s, 0:1, :] = jnp.full((1, width), -1e30, jnp.float32)
        stats[s, 1:3, :] = jnp.zeros((2, width), jnp.float32)

    def sub_of(s):
        return 2 * c + s * (31 - 4 * c)

    def last_of(s):
        return c + s * (15 - 2 * c)

    def first(s, p, block, masked):
        j = 2 * block + p
        place_at = s * (c + 1) + j
        m, l, d = stats[s, 0:1, :], stats[s, 1:2, :], stats[s, 2:3, :]
        scores = dot(kv[p, block, 0], qd[s, 0], NT) * (SCALE * LOG2E)
        dp = dot(kv[p, block, 1], qd[s, 1], NT)
        if masked:
            key_at = lax.broadcasted_iota(jnp.int32, (rows, width), 0) + j * rows
            query_at = lax.broadcasted_iota(jnp.int32, (rows, width), 1) % sub + sub_of(s) * sub
            scores = jnp.where(key_at <= query_at, scores, -jnp.inf)
        new = jnp.maximum(m, jnp.max(scores, axis=0, keepdims=True))
        factor = jnp.exp2(m - new)
        ex = jnp.exp2(scores - new)
        stats[s, 0:1, :] = new
        stats[s, 1:2, :] = l * factor + jnp.sum(ex, axis=0, keepdims=True)
        stats[s, 2:3, :] = d * factor + jnp.sum(ex * dp, axis=0, keepdims=True)
        probs[place_at] = ex.astype(probs.dtype)
        dprob[place_at] = dp
        maxes[place_at] = jnp.broadcast_to(new, (8, width))

    def second(s, p, block):
        j = 2 * block + p
        place_at = s * (c + 1) + j
        scale = jnp.exp2(maxes[place_at][0:1] - stats[s, 0:1, :]) * stats[s, 1:2, :]
        pr = probs[place_at].astype(jnp.float32) * scale
        ds = pr * (dprob[place_at] - stats[s, 2:3, :])
        p_b = pr.astype(jnp.bfloat16)
        ds_b = ds.astype(jnp.bfloat16)
        dkv[p, block, 0] += dot(ds_b, qd[s, 0], NN)
        dkv[p, block, 1] += dot(p_b, qd[s, 1], NN)
        dq_acc[s] += dot(kv[p, block, 0], ds_b, TN)

    def arrive(t):
        for n in range(2):
            first_hop(t, n).wait_recv()
            second_hop(t, n).start()

    def complete(t):
        for n in range(2):
            second_hop(t, n).wait_recv()
        relay(t).start()

    arrive(4)
    for t in range(5, 8):
        for n in range(2):
            first_hop(t, n).start()
    arrive(1)
    c_copy.wait()

    def first_step(t, carry):
        @pl.when((t + 2 < 8) & (t != 2))
        def _():
            arrive(t + 2)

        @pl.when(t + 1 < 8)
        def _():
            complete(t + 1)

        relay(t).wait_recv()
        block = from_chip(t)

        def tile(i, inner):
            s, p = i % 2, i // 2
            j = 2 * block + p

            @pl.when(j < last_of(s))
            def _():
                first(s, p, block, False)

            @pl.when(j == last_of(s))
            def _():
                first(s, p, block, True)

            return inner

        lax.fori_loop(0, 4, tile, 0)
        return carry

    lax.fori_loop(0, 8, first_step, 0)
    relay(0).wait_send()
    for t in range(1, 8):
        for n in range(2):
            first_hop(t, n).wait_send()
            second_hop(t, n).wait_send()
        relay(t).wait_send()

    for s in range(2):
        inverse = 1.0 / stats[s, 1:2, :]
        stats[s, 1:2, :] = inverse
        stats[s, 2:3, :] = stats[s, 2:3, :] * inverse

    far_core = 1 - core

    def merge(t):
        return remote(
            kv.at[far_core, to_chip(7 - t)],
            merge_recv.at[t],
            merge_sem.at[0, t],
            merge_sem.at[1, t],
            other_core,
        )

    def kept(t, n):
        return flip(z_lo, far_z(7 - t)) if n == 0 else y_half

    def mate_copy(t, n):
        return remote(
            kv.at[core, to_chip(7 - t), n, half(1 - kept(t, n)), :],
            e1_recv.at[t, n],
            e1_sem.at[0, t, n],
            e1_sem.at[1, t, n],
            z_mate if n == 0 else y_mate,
        )

    def ctx_copy(t):
        return remote(
            e2_send.at[t], e2_recv.at[t], e2_sem.at[0, t], e2_sem.at[1, t], to_device(7 - t)
        )

    def after_merge(t):
        block = to_chip(7 - t)
        merge(t).wait_recv()
        for n in range(2):
            there, here = half(1 - kept(t, n)), half(kept(t, n))
            kv[core, block, n, there, :] = (
                dkv[core, block, n, there, :] + merge_recv[t, n, there, :].astype(jnp.float32)
            ).astype(jnp.bfloat16)
            mate_copy(t, n).start()
            dkv[core, block, n, here, :] += merge_recv[t, n, here, :].astype(jnp.float32)

    def mate_sum(t, n):
        mate_copy(t, n).wait_recv()
        return dkv[core, to_chip(7 - t), n, half(kept(t, n)), :] + e1_recv[t, n].astype(
            jnp.float32
        )

    def after_mate(t):
        for n in range(2):
            e2_send[t, n] = mate_sum(t, n).astype(jnp.bfloat16)
        ctx_copy(t).start()

    def second_step(t, carry):
        block = to_chip(7 - t)

        def tile(i, inner):
            s, p = i % 2, i // 2

            @pl.when(2 * block + p <= last_of(s))
            def _():
                second(s, p, block)

            return inner

        lax.fori_loop(0, 4, tile, 0)
        kv[far_core, block] = dkv[far_core, block].astype(jnp.bfloat16)
        merge(t).start()

        @pl.when(t >= 2)
        def _():
            after_merge(t - 2)

        @pl.when(t >= 5)
        def _():
            after_mate(t - 5)

        return carry

    lax.fori_loop(0, 8, second_step, 0)
    after_merge(6)
    for s in range(2):
        dqs[s] = (dq_acc[s] * SCALE).T.astype(jnp.bfloat16)
    d_copy = remote(dqs.at[1], dq_recv, d_sem.at[0], d_sem.at[1], partner)
    d_copy.start()
    outs = []

    def store(src, dst):
        copy = pltpu.make_async_copy(src, dst, out_sem.at[len(outs)])
        copy.start()
        outs.append(copy)

    for h in range(heads):
        store(
            dqs.at[0, pl.ds(h * sub, sub), :], dq_ref.at[pl.ds(0, sub), pl.ds(h * HEAD, HEAD)]
        )
    after_mate(3)
    after_merge(7)
    for t in range(4, 7):
        after_mate(t)

    for copy in a_copies:
        copy.wait()
    weight_col = recv_rows[:, model : model + HEAD].astype(jnp.float32)
    weight_wide = jnp.concatenate([weight_col] * (chunk // HEAD), axis=1)

    def expert_step(i, score):
        slot = i % 2
        weight_copy(i, slot).wait()
        cols = pl.ds(pl.multiple_of(i * chunk, chunk), chunk)
        back = dot(recv_rows[:, 0:model], w_buf[slot], NT)

        @pl.when(i + 2 < chunks)
        def _():
            weight_copy(i + 2, slot).start()

        g = sg[:, cols].astype(jnp.float32)
        u = su[:, cols].astype(jnp.float32)
        sig = 1.0 / (1.0 + jnp.exp(-g))
        silu = g * sig
        act = (silu * u).astype(jnp.bfloat16).astype(jnp.float32)
        act_grad = weight_wide * back
        gp[:, cols] = (act_grad * u * sig * (1.0 + g * (1.0 - sig))).astype(jnp.bfloat16)
        up[:, cols] = (act_grad * silu).astype(jnp.bfloat16)
        return score + jnp.sum(act * back, axis=1, keepdims=True)

    score = lax.fori_loop(0, chunks, expert_step, jnp.zeros((slots, 1), jnp.float32))
    score_send[...] = jnp.broadcast_to(score, (slots, HEAD))
    score_copies = []
    for step in range(1, 8):
        far = (e + step) % 8
        copy = remote(
            score_send.at[far_rows(far), :],
            score_recv.at[own_rows, :],
            score_sem.at[0, step - 1],
            score_sem.at[1, step - 1],
            (c, far),
        )
        copy.start()
        score_copies.append(copy)
    score_recv[own_rows, :] = score_send[own_rows, :]
    store(gp, gp_ref)
    store(up, up_ref)

    for n in range(2):
        total[n] = mate_sum(7, n)
    for t in range(7):
        ctx_copy(t).wait_recv()
        total[...] += e2_recv[t].astype(jnp.float32)
    part = rows // 8

    def owner_copy(n, i):
        rows_i = pl.ds(i * part, part)
        if n == 0:
            return remote(
                total.at[0, rows_i, :], ebk.at[y], ebk_sem.at[0, i], ebk_sem.at[1, y], (c, 4 * z_lo + i)
            )
        source = (y // 2) * 2 + z_lo
        return remote(
            total.at[1, rows_i, :],
            ebv.at[source],
            ebv_sem.at[0, i],
            ebv_sem.at[1, source],
            (c, 4 * y_half + i),
        )

    def owner_of(n, i):
        return 4 * (z_lo if n == 0 else y_half) + i

    for n in range(2):
        for i in range(4):

            @pl.when(owner_of(n, i) != e)
            def _():
                owner_copy(n, i).start()

            @pl.when(owner_of(n, i) == e)
            def _():
                if n == 0:
                    ebk[y] = total[0, i * part : (i + 1) * part, :]
                else:
                    ebv[(y // 2) * 2 + z_lo] = total[1, i * part : (i + 1) * part, :]

    for copy in score_copies:
        copy.wait()
    picked = onehot[...] * score_recv[...]
    for k in range(TOPK):
        gg_out[k : k + 1, :] = jnp.sum(
            jnp.where(ids[k : k + 1, :] == slot_expert, picked, 0.0), axis=0, keepdims=True
        )
    store(gg_out, gg_ref)

    d_copy.wait()
    for h in range(heads):
        store(
            dq_recv.at[pl.ds(h * sub, sub), :],
            dq_ref.at[pl.ds(sub, sub), pl.ds(h * HEAD, HEAD)],
        )

    for i in range(4):
        source_k = 2 * i + e // 4
        source_v = (2 * (i // 2) + e // 4) * 2 + i % 2

        @pl.when(source_k != e)
        def _():
            remote(ebk.at[i], ebk.at[i], ebk_sem.at[0, i], ebk_sem.at[1, i], other_core).wait_recv()

        @pl.when(source_v != e)
        def _():
            remote(ebv.at[i], ebv.at[i], ebv_sem.at[0, i], ebv_sem.at[1, i], other_core).wait_recv()

    for kv_index in range(KVHEADS):
        cols = slice(kv_index * HEAD, (kv_index + 1) * HEAD)
        first_source = 2 * kv_index
        dk_out[:, cols] = ((ebk[first_source] + ebk[first_source + 1]) * SCALE).astype(jnp.bfloat16)
        dv_out[:, cols] = (ebv[first_source] + ebv[first_source + 1]).astype(jnp.bfloat16)
    store(dk_out, dk_ref)
    store(dv_out, dv_ref)

    for t in range(8):
        merge(t).wait_send()
        for n in range(2):
            mate_copy(t, n).wait_send()
        if t < 7:
            ctx_copy(t).wait_send()
    for n in range(2):
        for i in range(4):

            @pl.when(owner_of(n, i) != e)
            def _():
                owner_copy(n, i).wait_send()

    for copy in outs:
        copy.wait()


def hand_on(*refs):
    count = len(refs) // 2
    for n in range(count):
        refs[count + n][...] = refs[n][...]


def shards(
    queries,
    keys,
    values,
    out_grad,
    moe_grad,
    expert_ids,
    gate_weights,
    saved_gate,
    saved_up,
    down_weight,
):
    rows, columns = queries.shape
    sub = rows // 2
    width = columns // HEAD * sub
    tokens, model = moe_grad.shape
    slots, hidden = saved_gate.shape
    bf16, f32 = jnp.bfloat16, jnp.float32
    vmem = pl.BlockSpec(memory_space=pltpu.VMEM)
    hbm = pl.BlockSpec(memory_space=pl.ANY)
    dma = pltpu.SemaphoreType.DMA
    shapes = (
        jax.ShapeDtypeStruct((rows, columns), bf16),
        jax.ShapeDtypeStruct((rows // 8, KVHEADS * HEAD), bf16),
        jax.ShapeDtypeStruct((rows // 8, KVHEADS * HEAD), bf16),
        jax.ShapeDtypeStruct((TOPK, tokens), f32),
        jax.ShapeDtypeStruct((slots, hidden), bf16),
        jax.ShapeDtypeStruct((slots, hidden), bf16),
    )
    results = pl.pallas_call(
        body,
        out_shape=shapes,
        in_specs=[hbm] * 5 + [vmem] * 2 + [hbm] * 3,
        out_specs=(hbm,) * 6,
        scratch_shapes=[
            pltpu.VMEM((2, 8, 2, rows, HEAD), bf16),
            pltpu.VMEM((2, 2, width, HEAD), bf16),
            pltpu.VMEM((2, width, HEAD), bf16),
            pltpu.VMEM((17, rows, width), bf16),
            pltpu.VMEM((17, rows, width), f32),
            pltpu.VMEM((17, 8, width), f32),
            pltpu.VMEM((2, 8, width), f32),
            pltpu.VMEM((2, HEAD, width), f32),
            pltpu.VMEM((2, 8, 2, rows, HEAD), f32),
            pltpu.VMEM((2, width, HEAD), bf16),
            pltpu.VMEM((width, HEAD), bf16),
            pltpu.VMEM((8, 2, rows, HEAD), bf16),
            pltpu.VMEM((8, 2, sub, HEAD), bf16),
            pltpu.VMEM((7, 2, sub, HEAD), bf16),
            pltpu.VMEM((7, 2, sub, HEAD), bf16),
            pltpu.VMEM((2, sub, HEAD), f32),
            pltpu.VMEM((4, rows // 8, HEAD), f32),
            pltpu.VMEM((4, rows // 8, HEAD), f32),
            pltpu.VMEM((tokens, model), bf16),
            pltpu.VMEM((slots, model + HEAD), bf16),
            pltpu.VMEM((slots, model + HEAD), bf16),
            pltpu.VMEM((slots, tokens), f32),
            pltpu.VMEM((slots, HEAD), f32),
            pltpu.VMEM((slots, HEAD), f32),
            pltpu.VMEM((slots, hidden), bf16),
            pltpu.VMEM((slots, hidden), bf16),
            pltpu.VMEM((slots, hidden), bf16),
            pltpu.VMEM((slots, hidden), bf16),
            pltpu.VMEM((rows // 8, KVHEADS * HEAD), bf16),
            pltpu.VMEM((rows // 8, KVHEADS * HEAD), bf16),
            pltpu.VMEM((TOPK, tokens), f32),
            pltpu.VMEM((2, 256, model), bf16),
            dma((2,)),
            dma((21,)),
            dma((13,)),
            dma((2, 7)),
            dma((2, 8, 2)),
            dma((2, 8, 2)),
            dma((2, 8)),
            dma((2,)),
            dma((2,)),
            dma((2, 8)),
            dma((2, 8, 2)),
            dma((2, 7)),
            dma((2, 4)),
            dma((2, 4)),
            dma((2, 7)),
        ],
        compiler_params=pltpu.CompilerParams(
            collective_id=0, has_side_effects=True, vmem_limit_bytes=61 * 1024 * 1024
        ),
    )(
        queries,
        keys,
        values,
        out_grad,
        moe_grad,
        expert_ids.T,
        gate_weights.T,
        saved_gate,
        saved_up,
        down_weight,
    )
    results = pl.pallas_call(
        hand_on,
        out_shape=shapes,
        in_specs=[vmem] * 6,
        out_specs=(vmem,) * 6,
    )(*results)
    return results[0], results[1], results[2], results[3].T, results[4], results[5]


def solution(mesh):
    both = ("ctx", "exp")
    in_specs = (
        P("ctx", "exp"),
        P("ctx", None),
        P("ctx", None),
        P("ctx", "exp"),
        P(both, None),
        P(both, None),
        P(both, None),
        P(both, None),
        P(both, None),
        P("exp", None, None),
    )
    out_specs = (
        P("ctx", "exp"),
        P(both, None),
        P(both, None),
        P(both, None),
        P(both, None),
        P(both, None),
    )
    return jax.shard_map(shards, mesh=mesh, in_specs=in_specs, out_specs=out_specs, check_vma=False)
```

```python
import jax
import jax.numpy as jnp
from jax import lax
from jax.experimental import pallas as pl
from jax.experimental.pallas import tpu as pltpu
from jax.sharding import PartitionSpec as P

KVHEADS = 2
HEAD = 128
TOPK = 8
CAP = 16
LOG2E = 1.4426950408889634
SCALE = HEAD ** (-0.5)
MESH = pl.DeviceIdType.MESH
NT = (((1,), (1,)), ((), ()))
TN = (((0,), (0,)), ((), ()))
NN = (((1,), (0,)), ((), ()))


def dot(a, b, dims):
    return lax.dot_general(a, b, dims, preferred_element_type=jnp.float32)


def flip(a, b):
    return a + b - 2 * a * b


def body(
    q_ref,
    k_ref,
    v_ref,
    do_ref,
    moe_ref,
    ids_ref,
    gw_ref,
    sg_ref,
    su_ref,
    w_ref,
    dq_ref,
    dk_ref,
    dv_ref,
    gg_ref,
    gp_ref,
    up_ref,
    kv,
    qd,
    qd_send,
    probs,
    dprob,
    maxes,
    stats,
    dq_acc,
    dkv,
    dqs,
    dq_recv,
    merge_recv,
    e1_recv,
    e2_send,
    e2_recv,
    total,
    ebk,
    ebv,
    moe,
    send_rows,
    recv_rows,
    onehot,
    score_send,
    score_recv,
    sg,
    su,
    gp,
    up,
    dk_out,
    dv_out,
    gg_out,
    w_buf,
    w_sem,
    in_sem,
    out_sem,
    a_sem,
    s1_sem,
    s2_sem,
    relay_sem,
    c_sem,
    d_sem,
    merge_sem,
    e1_sem,
    e2_sem,
    ebk_sem,
    ebv_sem,
    score_sem,
):
    c = lax.axis_index("ctx")
    e = lax.axis_index("exp")
    rows = k_ref.shape[0]
    sub = rows // 2
    heads = q_ref.shape[1] // HEAD
    width = heads * sub
    tokens, model = moe_ref.shape
    slots, hidden = sg_ref.shape
    z_hi, x, core = c // 8, (c // 2) % 4, c % 2
    chip = c // 2
    y, z_lo = e // 2, e % 2
    y_half = y % 2
    kv_head = e // 4

    def far_z(t):
        return t // 4

    def shift(t):
        m = t % 4
        return m + m // 2 - 2 * (m // 3)

    def from_chip(t):
        return flip(z_hi, far_z(t)) * 4 + (x + 4 - shift(t)) % 4

    def to_chip(t):
        return flip(z_hi, far_z(t)) * 4 + (x + shift(t)) % 4

    def to_device(t):
        return (to_chip(t) * 2 + core, y * 2 + flip(z_lo, far_z(t)))

    other_core = (c + 1 - 2 * core, e)
    partner = (15 - c, y * 2 + 1 - z_lo)
    z_mate = (c, y * 2 + 1 - z_lo)
    y_mate = (c, (y + 1 - 2 * y_half) * 2 + z_lo)

    def remote(src, dst, send_sem, recv_sem, device):
        return pltpu.make_async_remote_copy(
            src_ref=src,
            dst_ref=dst,
            send_sem=send_sem,
            recv_sem=recv_sem,
            device_id=device,
            device_id_type=MESH,
        )

    def half(index):
        return pl.ds(pl.multiple_of(index * sub, sub), sub)

    barrier = pltpu.get_barrier_semaphore()
    peers = [to_device(t) for t in range(1, 5)]
    peers += [(c, (e + step) % 8) for step in range(1, 8)]
    peers += [other_core, partner]
    for peer in peers:
        pl.semaphore_signal(barrier, inc=1, device_id=peer, device_id_type=MESH)

    head_cols = pl.ds(pl.multiple_of(kv_head * HEAD, HEAD), HEAD)
    pairs = [
        (k_ref.at[:, head_cols], kv.at[core, chip, 0]),
        (v_ref.at[:, head_cols], kv.at[core, chip, 1]),
    ]
    for n, ref in enumerate((q_ref, do_ref)):
        for h in range(heads):
            cols = pl.ds(h * HEAD, HEAD)
            pairs.append((ref.at[pl.ds(sub, sub), cols], qd_send.at[n, pl.ds(h * sub, sub), :]))
    for n, ref in enumerate((q_ref, do_ref)):
        for h in range(heads):
            cols = pl.ds(h * HEAD, HEAD)
            pairs.append((ref.at[pl.ds(0, sub), cols], qd.at[0, n, pl.ds(h * sub, sub), :]))
    pairs += [(moe_ref, moe), (sg_ref, sg), (su_ref, su)]
    loads = [
        pltpu.make_async_copy(src, dst, in_sem.at[n]) for n, (src, dst) in enumerate(pairs)
    ]
    for load in loads[: 2 + 2 * heads]:
        load.start()
    loads[2 + 4 * heads].start()

    chunk = w_buf.shape[1]
    chunks = hidden // chunk

    def weight_copy(i, slot):
        return pltpu.make_async_copy(
            w_ref.at[0, pl.ds(pl.multiple_of(i * chunk, chunk), chunk), :],
            w_buf.at[slot],
            w_sem.at[slot],
        )

    dkv[...] = jnp.zeros_like(dkv)
    dq_acc[...] = jnp.zeros_like(dq_acc)
    for s in range(2):
        stats[s, 0:1, :] = jnp.full((1, width), -1e30, jnp.float32)
        stats[s, 1:3, :] = jnp.zeros((2, width), jnp.float32)

    for load in loads[: 2 + 2 * heads]:
        load.wait()
    pl.semaphore_wait(barrier, len(peers))

    wide = width // 2

    def exchange(part, n):
        piece = pl.ds(part * wide, wide)
        return remote(
            qd_send.at[n, piece, :],
            qd.at[1, n, piece, :],
            c_sem.at[0, part, n],
            c_sem.at[1, part, n],
            partner,
        )


    def first_hop(t, n):
        if isinstance(t, int) and t > 4:
            block, index = from_chip(4), 1 - z_lo if n == 0 else y_half
            device = ((chip - x + (x + shift(t)) % 4) * 2 + core, e)
        else:
            block, index = chip, z_lo if n == 0 else y_half
            device = to_device(t)
        piece = kv.at[core, block, n, half(index), :]
        return remote(piece, piece, s1_sem.at[0, t, n], s1_sem.at[1, t, n], device)

    def second_hop(t, n):
        index = flip(z_lo, far_z(t)) if n == 0 else y_half
        piece = kv.at[core, from_chip(t), n, half(index), :]
        mate = z_mate if n == 0 else y_mate
        return remote(piece, piece, s2_sem.at[0, t, n], s2_sem.at[1, t, n], mate)

    def relay(t):
        block = kv.at[core, from_chip(t)]
        return remote(block, block, relay_sem.at[0, t], relay_sem.at[1, t], other_core)

    for n in range(2):
        first_hop(4, n).start()
    for t in range(1, 4):
        for n in range(2):
            first_hop(t, n).start()
    relay(0).start()
    weight_copy(0, 0).start()
    weight_copy(1, 1).start()
    for load in loads[2 + 2 * heads : 2 + 4 * heads] + loads[3 + 4 * heads :]:
        load.start()

    slot_row = lax.broadcasted_iota(jnp.int32, (slots, tokens), 0)
    slot_expert = slot_row // CAP
    ids = ids_ref[...]
    weights = gw_ref[...].astype(jnp.float32)
    match = jnp.zeros((slots, tokens), jnp.float32)
    weight_of = jnp.zeros((slots, tokens), jnp.float32)
    for k in range(TOPK):
        hit = ids[k : k + 1, :] == slot_expert
        match = jnp.where(hit, 1.0, match)
        weight_of = jnp.where(hit, weights[k : k + 1, :], weight_of)
    row = lax.broadcasted_iota(jnp.int32, (tokens, tokens), 0)
    col = lax.broadcasted_iota(jnp.int32, (tokens, tokens), 1)
    earlier = jnp.where(row < col, 1.0, 0.0).astype(jnp.bfloat16)
    rank = dot(match.astype(jnp.bfloat16), earlier, NN)
    place = jnp.where(rank == (slot_row % CAP).astype(jnp.float32), match, 0.0)
    onehot[...] = place
    place_b = place.astype(jnp.bfloat16)
    loads[2 + 4 * heads].wait()
    step_cols = 512

    def gather_cols(i, carry):
        cols = pl.ds(pl.multiple_of(i * step_cols, step_cols), step_cols)
        send_rows[:, cols] = dot(place_b, moe[:, cols], NN).astype(jnp.bfloat16)
        return carry

    lax.fori_loop(0, model // step_cols, gather_cols, 0)
    slot_weight = dot(
        (place * weight_of).astype(jnp.bfloat16), jnp.ones((tokens, HEAD), jnp.bfloat16), NN
    )
    send_rows[:, model : model + HEAD] = slot_weight.astype(jnp.bfloat16)
    own_rows = pl.ds(pl.multiple_of(e * CAP, CAP), CAP)

    def far_rows(far):
        return pl.ds(pl.multiple_of(far * CAP, CAP), CAP)

    a_copies = []
    for step in range(1, 8):
        far = (e + step) % 8
        copy = remote(
            send_rows.at[far_rows(far), :],
            recv_rows.at[own_rows, :],
            a_sem.at[0, step - 1],
            a_sem.at[1, step - 1],
            (c, far),
        )
        a_copies.append(copy)
    recv_rows[own_rows, :] = send_rows[own_rows, :]

    def sub_of(s):
        return 2 * c + s * (31 - 4 * c)

    def last_of(s):
        return c + s * (15 - 2 * c)

    def last_pair(s):
        return last_of(s) // 2

    def first(s, block, cols, masked):
        place_at = 2 * (s * (c // 2 + 1) + block)
        m, l, d = stats[s, 0:1, cols], stats[s, 1:2, cols], stats[s, 2:3, cols]
        count = cols.stop - cols.start
        new = m
        scores, dprobs = [], []
        for p in range(2):
            sc = dot(kv[p, block, 0], qd[s, 0, cols, :], NT) * (SCALE * LOG2E)
            if masked:
                key_at = lax.broadcasted_iota(jnp.int32, (rows, count), 0)
                query_at = lax.broadcasted_iota(jnp.int32, (rows, count), 1) % sub
                offset = sub_of(s) * sub - (2 * block + p) * rows
                sc = jnp.where(key_at - query_at <= offset, sc, -jnp.inf)
            scores.append(sc)
            dprobs.append(dot(kv[p, block, 1], qd[s, 1, cols, :], NT))
            new = jnp.maximum(new, jnp.max(sc, axis=0, keepdims=True))
        factor = jnp.exp2(m - new)
        l = l * factor
        d = d * factor
        for p in range(2):
            ex = jnp.exp2(scores[p] - new)
            l = l + jnp.sum(ex, axis=0, keepdims=True)
            d = d + jnp.sum(ex * dprobs[p], axis=0, keepdims=True)
            probs[place_at + p, :, cols] = ex.astype(probs.dtype)
            dprob[place_at + p, :, cols] = dprobs[p]
        stats[s, 0:1, cols] = new
        stats[s, 1:2, cols] = l
        stats[s, 2:3, cols] = d
        maxes[s * (c // 2 + 1) + block, :, cols] = jnp.broadcast_to(new, (8, count))

    def first_pair(s, block, cols):
        @pl.when(block < last_pair(s))
        def _():
            first(s, block, cols, False)

        @pl.when(block == last_pair(s))
        def _():
            first(s, block, cols, True)

    def second(s, block):
        pair = s * (c // 2 + 1) + block
        scale = jnp.exp2(maxes[pair][0:1] - stats[s, 0:1, :]) * stats[s, 1:2, :]
        delta = stats[s, 2:3, :]
        dq = dq_acc[s]
        for p in range(2):
            pr = probs[2 * pair + p].astype(jnp.float32) * scale
            ds = pr * (dprob[2 * pair + p] - delta)
            p_b = pr.astype(jnp.bfloat16)
            ds_b = ds.astype(jnp.bfloat16)
            dkv[p, block, 0] += dot(ds_b, qd[s, 0], NN)
            dkv[p, block, 1] += dot(p_b, qd[s, 1], NN)
            dq = dq + dot(kv[p, block, 0], ds_b, TN)
        dq_acc[s] = dq

    def arrive(t):
        for n in range(2):
            first_hop(t, n).wait_recv()
            second_hop(t, n).start()

    def complete(t):
        for n in range(2):
            second_hop(t, n).wait_recv()
        relay(t).start()

    arrive(4)
    for t in range(5, 8):
        for n in range(2):
            first_hop(t, n).start()
    for t in range(1, 4):
        arrive(t)

    for part in range(2):
        for n in range(2):
            exchange(part, n).start()

    for load in loads[2 + 2 * heads : 2 + 4 * heads] + loads[3 + 4 * heads :]:
        load.wait()

    def first_step(i, carry):
        far = i // 8
        t = i % 4 + far * (4 + (i % 8) // 2 - i % 4)
        s = (i // 4) % 2 + far * (i % 2 - (i // 4) % 2)
        block = from_chip(t)

        @pl.when((i >= 1) & (i < 4))
        def _():
            arrive(i + 4)

        @pl.when(i < 7)
        def _():
            complete(i + 1)

        @pl.when((i < 4) | ((i >= 8) & (i % 2 == 0)))
        def _():
            relay(t).wait_recv()

        @pl.when(i == 4)
        def _():
            for n in range(2):
                exchange(0, n).wait()

        @pl.when(i == 7)
        def _():
            for copy in a_copies:
                copy.start()

        @pl.when(s == 0)
        def _():
            first_pair(0, block, slice(0, width))

        @pl.when(s == 1)
        def _():
            first_pair(1, block, slice(0, wide))

        return carry

    lax.fori_loop(0, 16, first_step, 0)
    for n in range(2):
        exchange(1, n).wait()

    def first_rest(t, carry):
        first_pair(1, t, slice(wide, width))
        return carry

    lax.fori_loop(0, 8, first_rest, 0)
    relay(0).wait_send()
    for t in range(1, 8):
        for n in range(2):
            first_hop(t, n).wait_send()
            second_hop(t, n).wait_send()
        relay(t).wait_send()

    for s in range(2):
        inverse = 1.0 / stats[s, 1:2, :]
        stats[s, 1:2, :] = inverse
        stats[s, 2:3, :] = stats[s, 2:3, :] * inverse

    far_core = 1 - core

    def merge(t):
        return remote(
            kv.at[far_core, to_chip(7 - t)],
            merge_recv.at[t],
            merge_sem.at[0, t],
            merge_sem.at[1, t],
            other_core,
        )

    def kept(t, n):
        return flip(z_lo, far_z(7 - t)) if n == 0 else y_half

    def mate_copy(t, n):
        return remote(
            kv.at[core, to_chip(7 - t), n, half(1 - kept(t, n)), :],
            e1_recv.at[t, n],
            e1_sem.at[0, t, n],
            e1_sem.at[1, t, n],
            z_mate if n == 0 else y_mate,
        )

    def ctx_copy(t):
        if isinstance(t, int) and t == 3:
            device = to_device(4)
        else:
            device = ((z_hi * 4 + (x + shift(7 - t)) % 4) * 2 + core, e)
        return remote(e2_send.at[t], e2_recv.at[t], e2_sem.at[0, t], e2_sem.at[1, t], device)

    def after_merge(t):
        block = to_chip(7 - t)
        merge(t).wait_recv()
        for n in range(2):
            there, here = half(1 - kept(t, n)), half(kept(t, n))
            kv[core, block, n, there, :] = (
                dkv[core, block, n, there, :] + merge_recv[t, n, there, :].astype(jnp.float32)
            ).astype(jnp.bfloat16)
            mate_copy(t, n).start()
            dkv[core, block, n, here, :] += merge_recv[t, n, here, :].astype(jnp.float32)

    def mate_sum(t, n):
        mate_copy(t, n).wait_recv()
        return dkv[core, to_chip(7 - t), n, half(kept(t, n)), :] + e1_recv[t, n].astype(
            jnp.float32
        )

    def after_mate(t):
        for n in range(2):
            e2_send[t, n] = mate_sum(t, n).astype(jnp.bfloat16)
        ctx_copy(t).start()

    def cross():
        sums = [mate_sum(3, n) for n in range(2)]
        for t in range(3):
            ctx_copy(t).wait_recv()
            for n in range(2):
                sums[n] = sums[n] + e2_recv[t, n].astype(jnp.float32)
        for n in range(2):
            e2_send[3, n] = sums[n].astype(jnp.bfloat16)
        ctx_copy(3).start()

    def second_step(t, carry):
        block = to_chip(7 - t)

        def tile(s, inner):
            @pl.when(block <= last_pair(s))
            def _():
                second(s, block)

            return inner

        lax.fori_loop(0, 2, tile, 0)
        kv[far_core, block] = dkv[far_core, block].astype(jnp.bfloat16)
        merge(t).start()

        @pl.when(t >= 2)
        def _():
            after_merge(t - 2)

        @pl.when((t >= 4) & (t < 7))
        def _():
            after_mate(t - 4)

        return carry

    lax.fori_loop(0, 8, second_step, 0)
    for s in range(1, -1, -1):
        dqs[s] = (dq_acc[s] * SCALE).T.astype(jnp.bfloat16)
        if s == 1:
            d_copy = remote(dqs.at[1], dq_recv, d_sem.at[0], d_sem.at[1], partner)
            d_copy.start()
    after_merge(6)
    after_mate(4)
    outs = []

    def store(src, dst):
        copy = pltpu.make_async_copy(src, dst, out_sem.at[len(outs)])
        copy.start()
        outs.append(copy)

    for h in range(heads):
        store(
            dqs.at[0, pl.ds(h * sub, sub), :], dq_ref.at[pl.ds(0, sub), pl.ds(h * HEAD, HEAD)]
        )

    for copy in a_copies:
        copy.wait()
    weight_col = recv_rows[:, model : model + HEAD].astype(jnp.float32)
    weight_wide = jnp.concatenate([weight_col] * (chunk // HEAD), axis=1)

    def expert_step(i, score):
        slot = i % 2
        weight_copy(i, slot).wait()
        cols = pl.ds(pl.multiple_of(i * chunk, chunk), chunk)
        back = dot(recv_rows[:, 0:model], w_buf[slot], NT)

        @pl.when(i + 2 < chunks)
        def _():
            weight_copy(i + 2, slot).start()

        g = sg[:, cols].astype(jnp.float32)
        u = su[:, cols].astype(jnp.float32)
        sig = 1.0 / (1.0 + jnp.exp(-g))
        silu = g * sig
        act = (silu * u).astype(jnp.bfloat16).astype(jnp.float32)
        act_grad = weight_wide * back
        gp[:, cols] = (act_grad * u * sig * (1.0 + g * (1.0 - sig))).astype(jnp.bfloat16)
        up[:, cols] = (act_grad * silu).astype(jnp.bfloat16)
        return score + jnp.sum(act * back, axis=1, keepdims=True)

    after_merge(7)
    score = lax.fori_loop(0, 2, expert_step, jnp.zeros((slots, 1), jnp.float32))
    cross()
    after_mate(5)
    score = lax.fori_loop(2, 4, expert_step, score)
    after_mate(6)
    score = lax.fori_loop(4, chunks, expert_step, score)
    score_send[...] = jnp.broadcast_to(score, (slots, HEAD))
    score_copies = []
    for step in range(1, 8):
        far = (e + step) % 8
        copy = remote(
            score_send.at[far_rows(far), :],
            score_recv.at[own_rows, :],
            score_sem.at[0, step - 1],
            score_sem.at[1, step - 1],
            (c, far),
        )
        copy.start()
        score_copies.append(copy)
    score_recv[own_rows, :] = score_send[own_rows, :]
    store(gp, gp_ref)
    store(up, up_ref)

    for n in range(2):
        total[n] = mate_sum(7, n)
    for t in range(3, 7):
        ctx_copy(t).wait_recv()
        total[...] += e2_recv[t].astype(jnp.float32)
    part = rows // 8

    def owner_copy(n, i):
        rows_i = pl.ds(i * part, part)
        if n == 0:
            return remote(
                total.at[0, rows_i, :], ebk.at[y], ebk_sem.at[0, i], ebk_sem.at[1, y], (c, 4 * z_lo + i)
            )
        source = (y // 2) * 2 + z_lo
        return remote(
            total.at[1, rows_i, :],
            ebv.at[source],
            ebv_sem.at[0, i],
            ebv_sem.at[1, source],
            (c, 4 * y_half + i),
        )

    def owner_of(n, i):
        return 4 * (z_lo if n == 0 else y_half) + i

    for n in range(2):
        for i in range(4):

            @pl.when(owner_of(n, i) != e)
            def _():
                owner_copy(n, i).start()

            @pl.when(owner_of(n, i) == e)
            def _():
                if n == 0:
                    ebk[y] = total[0, i * part : (i + 1) * part, :]
                else:
                    ebv[(y // 2) * 2 + z_lo] = total[1, i * part : (i + 1) * part, :]

    for copy in score_copies:
        copy.wait()
    picked = onehot[...] * score_recv[...]
    for k in range(TOPK):
        gg_out[k : k + 1, :] = jnp.sum(
            jnp.where(ids[k : k + 1, :] == slot_expert, picked, 0.0), axis=0, keepdims=True
        )
    store(gg_out, gg_ref)

    d_copy.wait()
    for h in range(heads):
        store(
            dq_recv.at[pl.ds(h * sub, sub), :],
            dq_ref.at[pl.ds(sub, sub), pl.ds(h * HEAD, HEAD)],
        )

    for i in range(4):
        source_k = 2 * i + e // 4
        source_v = (2 * (i // 2) + e // 4) * 2 + i % 2

        @pl.when(source_k != e)
        def _():
            remote(ebk.at[i], ebk.at[i], ebk_sem.at[0, i], ebk_sem.at[1, i], other_core).wait_recv()

        @pl.when(source_v != e)
        def _():
            remote(ebv.at[i], ebv.at[i], ebv_sem.at[0, i], ebv_sem.at[1, i], other_core).wait_recv()

    for kv_index in range(KVHEADS):
        cols = slice(kv_index * HEAD, (kv_index + 1) * HEAD)
        first_source = 2 * kv_index
        dk_out[:, cols] = ((ebk[first_source] + ebk[first_source + 1]) * SCALE).astype(jnp.bfloat16)
        dv_out[:, cols] = (ebv[first_source] + ebv[first_source + 1]).astype(jnp.bfloat16)
    store(dk_out, dk_ref)
    store(dv_out, dv_ref)

    for t in range(8):
        merge(t).wait_send()
        for n in range(2):
            mate_copy(t, n).wait_send()
        if t < 7:
            ctx_copy(t).wait_send()
    for n in range(2):
        for i in range(4):

            @pl.when(owner_of(n, i) != e)
            def _():
                owner_copy(n, i).wait_send()

    for copy in outs:
        copy.wait()


def hand_on(*refs):
    count = len(refs) // 2
    for n in range(count):
        refs[count + n][...] = refs[n][...]


def shards(
    queries,
    keys,
    values,
    out_grad,
    moe_grad,
    expert_ids,
    gate_weights,
    saved_gate,
    saved_up,
    down_weight,
):
    rows, columns = queries.shape
    sub = rows // 2
    width = columns // HEAD * sub
    tokens, model = moe_grad.shape
    slots, hidden = saved_gate.shape
    bf16, f32 = jnp.bfloat16, jnp.float32
    vmem = pl.BlockSpec(memory_space=pltpu.VMEM)
    hbm = pl.BlockSpec(memory_space=pl.ANY)
    dma = pltpu.SemaphoreType.DMA
    shapes = (
        jax.ShapeDtypeStruct((rows, columns), bf16),
        jax.ShapeDtypeStruct((rows // 8, KVHEADS * HEAD), bf16),
        jax.ShapeDtypeStruct((rows // 8, KVHEADS * HEAD), bf16),
        jax.ShapeDtypeStruct((TOPK, tokens), f32),
        jax.ShapeDtypeStruct((slots, hidden), bf16),
        jax.ShapeDtypeStruct((slots, hidden), bf16),
    )
    results = pl.pallas_call(
        body,
        out_shape=shapes,
        in_specs=[hbm] * 5 + [vmem] * 2 + [hbm] * 3,
        out_specs=(hbm,) * 6,
        scratch_shapes=[
            pltpu.VMEM((2, 8, 2, rows, HEAD), bf16),
            pltpu.VMEM((2, 2, width, HEAD), bf16),
            pltpu.VMEM((2, width, HEAD), bf16),
            pltpu.VMEM((18, rows, width), bf16),
            pltpu.VMEM((18, rows, width), f32),
            pltpu.VMEM((9, 8, width), f32),
            pltpu.VMEM((2, 8, width), f32),
            pltpu.VMEM((2, HEAD, width), f32),
            pltpu.VMEM((2, 8, 2, rows, HEAD), f32),
            pltpu.VMEM((2, width, HEAD), bf16),
            pltpu.VMEM((width, HEAD), bf16),
            pltpu.VMEM((8, 2, rows, HEAD), bf16),
            pltpu.VMEM((8, 2, sub, HEAD), bf16),
            pltpu.VMEM((7, 2, sub, HEAD), bf16),
            pltpu.VMEM((7, 2, sub, HEAD), bf16),
            pltpu.VMEM((2, sub, HEAD), f32),
            pltpu.VMEM((4, rows // 8, HEAD), f32),
            pltpu.VMEM((4, rows // 8, HEAD), f32),
            pltpu.VMEM((tokens, model), bf16),
            pltpu.VMEM((slots, model + HEAD), bf16),
            pltpu.VMEM((slots, model + HEAD), bf16),
            pltpu.VMEM((slots, tokens), f32),
            pltpu.VMEM((slots, HEAD), f32),
            pltpu.VMEM((slots, HEAD), f32),
            pltpu.VMEM((slots, hidden), bf16),
            pltpu.VMEM((slots, hidden), bf16),
            pltpu.VMEM((slots, hidden), bf16),
            pltpu.VMEM((slots, hidden), bf16),
            pltpu.VMEM((rows // 8, KVHEADS * HEAD), bf16),
            pltpu.VMEM((rows // 8, KVHEADS * HEAD), bf16),
            pltpu.VMEM((TOPK, tokens), f32),
            pltpu.VMEM((2, 256, model), bf16),
            dma((2,)),
            dma((21,)),
            dma((13,)),
            dma((2, 7)),
            dma((2, 8, 2)),
            dma((2, 8, 2)),
            dma((2, 8)),
            dma((2, 2, 2)),
            dma((2,)),
            dma((2, 8)),
            dma((2, 8, 2)),
            dma((2, 7)),
            dma((2, 4)),
            dma((2, 4)),
            dma((2, 7)),
        ],
        compiler_params=pltpu.CompilerParams(
            collective_id=0, has_side_effects=True, vmem_limit_bytes=61 * 1024 * 1024
        ),
    )(
        queries,
        keys,
        values,
        out_grad,
        moe_grad,
        expert_ids.T,
        gate_weights.T,
        saved_gate,
        saved_up,
        down_weight,
    )
    results = pl.pallas_call(
        hand_on,
        out_shape=shapes,
        in_specs=[vmem] * 6,
        out_specs=(vmem,) * 6,
    )(*results)
    return results[0], results[1], results[2], results[3].T, results[4], results[5]


def solution(mesh):
    both = ("ctx", "exp")
    in_specs = (
        P("ctx", "exp"),
        P("ctx", None),
        P("ctx", None),
        P("ctx", "exp"),
        P(both, None),
        P(both, None),
        P(both, None),
        P(both, None),
        P(both, None),
        P("exp", None, None),
    )
    out_specs = (
        P("ctx", "exp"),
        P(both, None),
        P(both, None),
        P(both, None),
        P(both, None),
        P(both, None),
    )
    return jax.shard_map(shards, mesh=mesh, in_specs=in_specs, out_specs=out_specs, check_vma=False)
```

```python
import jax
import jax.numpy as jnp
from jax import lax
from jax.experimental import pallas as pl
from jax.experimental.pallas import tpu as pltpu
from jax.sharding import PartitionSpec as P

KVHEADS = 2
HEAD = 128
TOPK = 8
CAP = 16
LOG2E = 1.4426950408889634
SCALE = HEAD ** (-0.5)
MESH = pl.DeviceIdType.MESH
NT = (((1,), (1,)), ((), ()))
TN = (((0,), (0,)), ((), ()))
NN = (((1,), (0,)), ((), ()))


def dot(a, b, dims):
    return lax.dot_general(a, b, dims, preferred_element_type=jnp.float32)


def flip(a, b):
    return a + b - 2 * a * b


def body(
    q_ref,
    k_ref,
    v_ref,
    do_ref,
    moe_ref,
    ids_ref,
    gw_ref,
    sg_ref,
    su_ref,
    w_ref,
    dq_ref,
    dk_ref,
    dv_ref,
    gg_ref,
    gp_ref,
    up_ref,
    kv,
    qd,
    qd_send,
    probs,
    dprob,
    maxes,
    stats,
    dq_acc,
    dkv,
    dqs,
    merge_recv,
    e1_recv,
    e2_send,
    e2_recv,
    total,
    ebk,
    ebv,
    moe,
    send_rows,
    recv_rows,
    onehot,
    score_send,
    score_recv,
    sg,
    su,
    gp,
    up,
    dk_out,
    dv_out,
    gg_out,
    w_buf,
    w_sem,
    in_sem,
    out_sem,
    a_sem,
    s1_sem,
    s2_sem,
    relay_sem,
    c_sem,
    d_sem,
    merge_sem,
    e1_sem,
    e2_sem,
    ebk_sem,
    ebv_sem,
    score_sem,
):
    c = lax.axis_index("ctx")
    e = lax.axis_index("exp")
    rows = k_ref.shape[0]
    sub = rows // 2
    heads = q_ref.shape[1] // HEAD
    width = heads * sub
    tokens, model = moe_ref.shape
    slots, hidden = sg_ref.shape
    z_hi, x, core = c // 8, (c // 2) % 4, c % 2
    chip = c // 2
    y, z_lo = e // 2, e % 2
    y_half = y % 2
    kv_head = e // 4

    def far_z(t):
        return t // 4

    def shift(t):
        m = t % 4
        return m + m // 2 - 2 * (m // 3)

    def from_chip(t):
        return flip(z_hi, far_z(t)) * 4 + (x + 4 - shift(t)) % 4

    def to_chip(t):
        return flip(z_hi, far_z(t)) * 4 + (x + shift(t)) % 4

    def to_device(t):
        return (to_chip(t) * 2 + core, y * 2 + flip(z_lo, far_z(t)))

    other_core = (c + 1 - 2 * core, e)
    partner = (15 - c, y * 2 + 1 - z_lo)
    z_mate = (c, y * 2 + 1 - z_lo)
    y_mate = (c, (y + 1 - 2 * y_half) * 2 + z_lo)

    def remote(src, dst, send_sem, recv_sem, device):
        return pltpu.make_async_remote_copy(
            src_ref=src,
            dst_ref=dst,
            send_sem=send_sem,
            recv_sem=recv_sem,
            device_id=device,
            device_id_type=MESH,
        )

    def half(index):
        return pl.ds(pl.multiple_of(index * sub, sub), sub)

    barrier = pltpu.get_barrier_semaphore()
    peers = [to_device(t) for t in range(1, 5)]
    peers += [(c, (e + step) % 8) for step in range(1, 8)]
    peers += [other_core, partner]
    for peer in peers:
        pl.semaphore_signal(barrier, inc=1, device_id=peer, device_id_type=MESH)

    head_cols = pl.ds(pl.multiple_of(kv_head * HEAD, HEAD), HEAD)
    pairs = [
        (k_ref.at[:, head_cols], kv.at[core, chip, 0]),
        (v_ref.at[:, head_cols], kv.at[core, chip, 1]),
    ]
    for n, ref in enumerate((q_ref, do_ref)):
        for h in range(heads):
            cols = pl.ds(h * HEAD, HEAD)
            pairs.append((ref.at[pl.ds(sub, sub), cols], qd_send.at[n, pl.ds(h * sub, sub), :]))
    for n, ref in enumerate((q_ref, do_ref)):
        for h in range(heads):
            cols = pl.ds(h * HEAD, HEAD)
            pairs.append((ref.at[pl.ds(0, sub), cols], qd.at[0, n, pl.ds(h * sub, sub), :]))
    pairs += [(moe_ref, moe), (sg_ref, sg), (su_ref, su)]
    loads = [
        pltpu.make_async_copy(src, dst, in_sem.at[n]) for n, (src, dst) in enumerate(pairs)
    ]
    for load in loads[: 2 + 2 * heads]:
        load.start()
    loads[2 + 4 * heads].start()

    chunk = w_buf.shape[1]
    chunks = hidden // chunk

    def weight_copy(i, slot):
        return pltpu.make_async_copy(
            w_ref.at[0, pl.ds(pl.multiple_of(i * chunk, chunk), chunk), :],
            w_buf.at[slot],
            w_sem.at[slot],
        )

    dkv[...] = jnp.zeros_like(dkv)
    dq_acc[...] = jnp.zeros_like(dq_acc)
    for s in range(2):
        stats[s, 0:1, :] = jnp.full((1, width), -1e30, jnp.float32)
        stats[s, 1:3, :] = jnp.zeros((2, width), jnp.float32)

    for load in loads[: 2 + 2 * heads]:
        load.wait()
    pl.semaphore_wait(barrier, len(peers))

    wide = width // 2

    def exchange(part, n):
        piece = pl.ds(part * wide, wide)
        return remote(
            qd_send.at[n, piece, :],
            qd.at[1, n, piece, :],
            c_sem.at[0, part, n],
            c_sem.at[1, part, n],
            partner,
        )


    def first_hop(t, n):
        if isinstance(t, int) and t > 4:
            block, index = from_chip(4), 1 - z_lo if n == 0 else y_half
            device = ((chip - x + (x + shift(t)) % 4) * 2 + core, e)
        else:
            block, index = chip, z_lo if n == 0 else y_half
            device = to_device(t)
        piece = kv.at[core, block, n, half(index), :]
        return remote(piece, piece, s1_sem.at[0, t, n], s1_sem.at[1, t, n], device)

    def second_hop(t, n):
        index = flip(z_lo, far_z(t)) if n == 0 else y_half
        piece = kv.at[core, from_chip(t), n, half(index), :]
        mate = z_mate if n == 0 else y_mate
        return remote(piece, piece, s2_sem.at[0, t, n], s2_sem.at[1, t, n], mate)

    def relay(t):
        block = kv.at[core, from_chip(t)]
        return remote(block, block, relay_sem.at[0, t], relay_sem.at[1, t], other_core)

    for n in range(2):
        first_hop(4, n).start()
    for t in range(1, 4):
        for n in range(2):
            first_hop(t, n).start()
    relay(0).start()
    weight_copy(0, 0).start()
    weight_copy(1, 1).start()
    for load in loads[2 + 2 * heads : 2 + 4 * heads] + loads[3 + 4 * heads :]:
        load.start()

    slot_row = lax.broadcasted_iota(jnp.int32, (slots, tokens), 0)
    slot_expert = slot_row // CAP
    ids = ids_ref[...]
    def route():
        weights = gw_ref[...].astype(jnp.float32)
        match = jnp.zeros((slots, tokens), jnp.float32)
        weight_of = jnp.zeros((slots, tokens), jnp.float32)
        for k in range(TOPK):
            hit = ids[k : k + 1, :] == slot_expert
            match = jnp.where(hit, 1.0, match)
            weight_of = jnp.where(hit, weights[k : k + 1, :], weight_of)
        row = lax.broadcasted_iota(jnp.int32, (tokens, tokens), 0)
        col = lax.broadcasted_iota(jnp.int32, (tokens, tokens), 1)
        earlier = jnp.where(row < col, 1.0, 0.0).astype(jnp.bfloat16)
        rank = dot(match.astype(jnp.bfloat16), earlier, NN)
        place = jnp.where(rank == (slot_row % CAP).astype(jnp.float32), match, 0.0)
        onehot[...] = place
        place_b = place.astype(jnp.bfloat16)
        loads[2 + 4 * heads].wait()
        step_cols = 512

        def gather_cols(i, carry):
            cols = pl.ds(pl.multiple_of(i * step_cols, step_cols), step_cols)
            send_rows[:, cols] = dot(place_b, moe[:, cols], NN).astype(jnp.bfloat16)
            return carry

        lax.fori_loop(0, model // step_cols, gather_cols, 0)
        slot_weight = dot(
            (place * weight_of).astype(jnp.bfloat16), jnp.ones((tokens, HEAD), jnp.bfloat16), NN
        )
        send_rows[:, model : model + HEAD] = slot_weight.astype(jnp.bfloat16)
    own_rows = pl.ds(pl.multiple_of(e * CAP, CAP), CAP)

    def far_rows(far):
        return pl.ds(pl.multiple_of(far * CAP, CAP), CAP)

    a_copies = []
    for step in range(1, 8):
        far = (e + step) % 8
        copy = remote(
            send_rows.at[far_rows(far), :],
            recv_rows.at[own_rows, :],
            a_sem.at[0, step - 1],
            a_sem.at[1, step - 1],
            (c, far),
        )
        a_copies.append(copy)

    def sub_of(s):
        return 2 * c + s * (31 - 4 * c)

    def last_of(s):
        return c + s * (15 - 2 * c)

    def last_pair(s):
        return last_of(s) // 2

    def first(s, block, cols, masked):
        place_at = 2 * (s * (c // 2 + 1) + block)
        m, l, d = stats[s, 0:1, cols], stats[s, 1:2, cols], stats[s, 2:3, cols]
        count = cols.stop - cols.start
        new = m
        scores, dprobs = [], []
        for p in range(2):
            sc = dot(kv[p, block, 0], qd[s, 0, cols, :], NT) * (SCALE * LOG2E)
            if masked:
                key_at = lax.broadcasted_iota(jnp.int32, (rows, count), 0)
                query_at = lax.broadcasted_iota(jnp.int32, (rows, count), 1) % sub
                offset = sub_of(s) * sub - (2 * block + p) * rows
                sc = jnp.where(key_at - query_at <= offset, sc, -jnp.inf)
            scores.append(sc)
            dprobs.append(dot(kv[p, block, 1], qd[s, 1, cols, :], NT))
            new = jnp.maximum(new, jnp.max(sc, axis=0, keepdims=True))
        factor = jnp.exp2(m - new)
        l = l * factor
        d = d * factor
        for p in range(2):
            ex = jnp.exp2(scores[p] - new)
            l = l + jnp.sum(ex, axis=0, keepdims=True)
            d = d + jnp.sum(ex * dprobs[p], axis=0, keepdims=True)
            probs[place_at + p, :, cols] = ex.astype(probs.dtype)
            dprob[place_at + p, :, cols] = dprobs[p]
        stats[s, 0:1, cols] = new
        stats[s, 1:2, cols] = l
        stats[s, 2:3, cols] = d
        maxes[s * (c // 2 + 1) + block, :, cols] = jnp.broadcast_to(new, (8, count))

    def first_pair(s, block, cols):
        @pl.when(block < last_pair(s))
        def _():
            first(s, block, cols, False)

        @pl.when(block == last_pair(s))
        def _():
            first(s, block, cols, True)

    def second(s, block):
        pair = s * (c // 2 + 1) + block
        scale = jnp.exp2(maxes[pair][0:1] - stats[s, 0:1, :]) * stats[s, 1:2, :]
        delta = stats[s, 2:3, :]
        dq = dq_acc[s]
        for p in range(2):
            pr = probs[2 * pair + p].astype(jnp.float32) * scale
            ds = pr * (dprob[2 * pair + p] - delta)
            p_b = pr.astype(jnp.bfloat16)
            ds_b = ds.astype(jnp.bfloat16)
            dkv[p, block, 0] += dot(ds_b, qd[s, 0], NN)
            dkv[p, block, 1] += dot(p_b, qd[s, 1], NN)
            dq = dq + dot(kv[p, block, 0], ds_b, TN)
        dq_acc[s] = dq

    def arrive(t):
        for n in range(2):
            first_hop(t, n).wait_recv()
            second_hop(t, n).start()

    def complete(t):
        for n in range(2):
            second_hop(t, n).wait_recv()
        relay(t).start()

    arrive(4)
    for t in range(5, 8):
        for n in range(2):
            first_hop(t, n).start()
    for t in range(1, 4):
        arrive(t)

    for part in range(2):
        for n in range(2):
            exchange(part, n).start()

    for load in loads[2 + 2 * heads : 2 + 4 * heads] + loads[3 + 4 * heads :]:
        load.wait()

    def first_step(i, carry):
        far = i // 8
        t = i % 4 + far * (4 + (i % 8) // 2 - i % 4)
        s = (i // 4) % 2 + far * (i % 2 - (i // 4) % 2)
        block = from_chip(t)

        @pl.when((i >= 1) & (i < 4))
        def _():
            arrive(i + 4)

        @pl.when(i < 7)
        def _():
            complete(i + 1)

        @pl.when((i < 4) | ((i >= 8) & (i % 2 == 0)))
        def _():
            relay(t).wait_recv()

        @pl.when(i == 4)
        def _():
            route()
            recv_rows[own_rows, :] = send_rows[own_rows, :]
            for copy in a_copies:
                copy.start()
            for n in range(2):
                exchange(0, n).wait()

        @pl.when(s == 0)
        def _():
            first_pair(0, block, slice(0, width))

        @pl.when(s == 1)
        def _():
            first_pair(1, block, slice(0, wide))

        return carry

    lax.fori_loop(0, 16, first_step, 0)
    for n in range(2):
        exchange(1, n).wait()

    def first_rest(t, carry):
        first_pair(1, t, slice(wide, width))
        return carry

    lax.fori_loop(0, 8, first_rest, 0)
    relay(0).wait_send()
    for t in range(1, 8):
        for n in range(2):
            first_hop(t, n).wait_send()
            second_hop(t, n).wait_send()
        relay(t).wait_send()

    for s in range(2):
        inverse = 1.0 / stats[s, 1:2, :]
        stats[s, 1:2, :] = inverse
        stats[s, 2:3, :] = stats[s, 2:3, :] * inverse

    far_core = 1 - core

    def merge(t):
        return remote(
            kv.at[far_core, to_chip(7 - t)],
            merge_recv.at[t],
            merge_sem.at[0, t],
            merge_sem.at[1, t],
            other_core,
        )

    def kept(t, n):
        return flip(z_lo, far_z(7 - t)) if n == 0 else y_half

    def mate_copy(t, n):
        return remote(
            kv.at[core, to_chip(7 - t), n, half(1 - kept(t, n)), :],
            e1_recv.at[t, n],
            e1_sem.at[0, t, n],
            e1_sem.at[1, t, n],
            z_mate if n == 0 else y_mate,
        )

    def ctx_copy(t):
        if isinstance(t, int) and t == 3:
            device = to_device(4)
        else:
            device = ((z_hi * 4 + (x + shift(7 - t)) % 4) * 2 + core, e)
        return remote(e2_send.at[t], e2_recv.at[t], e2_sem.at[0, t], e2_sem.at[1, t], device)

    def after_merge(t):
        block = to_chip(7 - t)
        merge(t).wait_recv()
        for n in range(2):
            there, here = half(1 - kept(t, n)), half(kept(t, n))
            kv[core, block, n, there, :] = (
                dkv[core, block, n, there, :] + merge_recv[t, n, there, :].astype(jnp.float32)
            ).astype(jnp.bfloat16)
            mate_copy(t, n).start()
            dkv[core, block, n, here, :] += merge_recv[t, n, here, :].astype(jnp.float32)

    def mate_sum(t, n):
        mate_copy(t, n).wait_recv()
        return dkv[core, to_chip(7 - t), n, half(kept(t, n)), :] + e1_recv[t, n].astype(
            jnp.float32
        )

    def after_mate(t):
        for n in range(2):
            e2_send[t, n] = mate_sum(t, n).astype(jnp.bfloat16)
        ctx_copy(t).start()

    def cross():
        sums = [mate_sum(3, n) for n in range(2)]
        for t in range(3):
            ctx_copy(t).wait_recv()
            for n in range(2):
                sums[n] = sums[n] + e2_recv[t, n].astype(jnp.float32)
        for n in range(2):
            e2_send[3, n] = sums[n].astype(jnp.bfloat16)
        ctx_copy(3).start()

    def second_step(t, carry):
        block = to_chip(7 - t)

        def tile(s, inner):
            @pl.when(block <= last_pair(s))
            def _():
                second(s, block)

            return inner

        lax.fori_loop(0, 2, tile, 0)
        kv[far_core, block] = dkv[far_core, block].astype(jnp.bfloat16)
        merge(t).start()

        @pl.when(t >= 2)
        def _():
            after_merge(t - 2)

        @pl.when((t >= 4) & (t < 7))
        def _():
            after_mate(t - 4)

        return carry

    lax.fori_loop(0, 8, second_step, 0)
    for s in range(1, -1, -1):
        dqs[s] = (dq_acc[s] * SCALE).T.astype(jnp.bfloat16)
        if s == 1:
            d_copies = [
                remote(
                    dqs.at[1, pl.ds(h * sub, sub), :],
                    dq_ref.at[pl.ds(sub, sub), pl.ds(h * HEAD, HEAD)],
                    d_sem.at[0, h],
                    d_sem.at[1, h],
                    partner,
                )
                for h in range(heads)
            ]
            for copy in d_copies:
                copy.start()
    after_merge(6)
    after_mate(4)
    outs = []

    def store(src, dst):
        copy = pltpu.make_async_copy(src, dst, out_sem.at[len(outs)])
        copy.start()
        outs.append(copy)

    for h in range(heads):
        store(
            dqs.at[0, pl.ds(h * sub, sub), :], dq_ref.at[pl.ds(0, sub), pl.ds(h * HEAD, HEAD)]
        )

    for copy in a_copies:
        copy.wait()
    weight_col = recv_rows[:, model : model + HEAD].astype(jnp.float32)
    weight_wide = jnp.concatenate([weight_col] * (chunk // HEAD), axis=1)

    def expert_step(i, score):
        slot = i % 2
        weight_copy(i, slot).wait()
        cols = pl.ds(pl.multiple_of(i * chunk, chunk), chunk)
        back = dot(recv_rows[:, 0:model], w_buf[slot], NT)

        @pl.when(i + 2 < chunks)
        def _():
            weight_copy(i + 2, slot).start()

        g = sg[:, cols].astype(jnp.float32)
        u = su[:, cols].astype(jnp.float32)
        sig = 1.0 / (1.0 + jnp.exp(-g))
        silu = g * sig
        act = (silu * u).astype(jnp.bfloat16).astype(jnp.float32)
        act_grad = weight_wide * back
        gp[:, cols] = (act_grad * u * sig * (1.0 + g * (1.0 - sig))).astype(jnp.bfloat16)
        up[:, cols] = (act_grad * silu).astype(jnp.bfloat16)
        return score + jnp.sum(act * back, axis=1, keepdims=True)

    after_merge(7)
    score = lax.fori_loop(0, 2, expert_step, jnp.zeros((slots, 1), jnp.float32))
    cross()
    after_mate(5)
    score = lax.fori_loop(2, 4, expert_step, score)
    after_mate(6)
    score = lax.fori_loop(4, chunks, expert_step, score)
    score_send[...] = jnp.broadcast_to(score, (slots, HEAD))
    score_copies = []
    for step in range(1, 8):
        far = (e + step) % 8
        copy = remote(
            score_send.at[far_rows(far), :],
            score_recv.at[own_rows, :],
            score_sem.at[0, step - 1],
            score_sem.at[1, step - 1],
            (c, far),
        )
        copy.start()
        score_copies.append(copy)
    score_recv[own_rows, :] = score_send[own_rows, :]
    store(gp, gp_ref)
    store(up, up_ref)

    for n in range(2):
        total[n] = mate_sum(7, n)
    for t in range(3, 7):
        ctx_copy(t).wait_recv()
        total[...] += e2_recv[t].astype(jnp.float32)
    part = rows // 8

    def owner_copy(n, i):
        rows_i = pl.ds(i * part, part)
        if n == 0:
            return remote(
                total.at[0, rows_i, :], ebk.at[y], ebk_sem.at[0, i], ebk_sem.at[1, y], (c, 4 * z_lo + i)
            )
        source = (y // 2) * 2 + z_lo
        return remote(
            total.at[1, rows_i, :],
            ebv.at[source],
            ebv_sem.at[0, i],
            ebv_sem.at[1, source],
            (c, 4 * y_half + i),
        )

    def owner_of(n, i):
        return 4 * (z_lo if n == 0 else y_half) + i

    for n in range(2):
        for i in range(4):

            @pl.when(owner_of(n, i) != e)
            def _():
                owner_copy(n, i).start()

            @pl.when(owner_of(n, i) == e)
            def _():
                if n == 0:
                    ebk[y] = total[0, i * part : (i + 1) * part, :]
                else:
                    ebv[(y // 2) * 2 + z_lo] = total[1, i * part : (i + 1) * part, :]

    for copy in score_copies:
        copy.wait()
    picked = onehot[...] * score_recv[...]
    for k in range(TOPK):
        gg_out[k : k + 1, :] = jnp.sum(
            jnp.where(ids[k : k + 1, :] == slot_expert, picked, 0.0), axis=0, keepdims=True
        )
    store(gg_out, gg_ref)

    for i in range(4):
        source_k = 2 * i + e // 4
        source_v = (2 * (i // 2) + e // 4) * 2 + i % 2

        @pl.when(source_k != e)
        def _():
            remote(ebk.at[i], ebk.at[i], ebk_sem.at[0, i], ebk_sem.at[1, i], other_core).wait_recv()

        @pl.when(source_v != e)
        def _():
            remote(ebv.at[i], ebv.at[i], ebv_sem.at[0, i], ebv_sem.at[1, i], other_core).wait_recv()

    for kv_index in range(KVHEADS):
        cols = slice(kv_index * HEAD, (kv_index + 1) * HEAD)
        first_source = 2 * kv_index
        dk_out[:, cols] = ((ebk[first_source] + ebk[first_source + 1]) * SCALE).astype(jnp.bfloat16)
        dv_out[:, cols] = (ebv[first_source] + ebv[first_source + 1]).astype(jnp.bfloat16)
    store(dk_out, dk_ref)
    store(dv_out, dv_ref)

    for t in range(8):
        merge(t).wait_send()
        for n in range(2):
            mate_copy(t, n).wait_send()
        if t < 7:
            ctx_copy(t).wait_send()
    for n in range(2):
        for i in range(4):

            @pl.when(owner_of(n, i) != e)
            def _():
                owner_copy(n, i).wait_send()

    for copy in d_copies + outs:
        copy.wait()


def hand_on(*refs):
    count = len(refs) // 2
    for n in range(count):
        refs[count + n][...] = refs[n][...]


def shards(
    queries,
    keys,
    values,
    out_grad,
    moe_grad,
    expert_ids,
    gate_weights,
    saved_gate,
    saved_up,
    down_weight,
):
    rows, columns = queries.shape
    sub = rows // 2
    width = columns // HEAD * sub
    tokens, model = moe_grad.shape
    slots, hidden = saved_gate.shape
    bf16, f32 = jnp.bfloat16, jnp.float32
    vmem = pl.BlockSpec(memory_space=pltpu.VMEM)
    hbm = pl.BlockSpec(memory_space=pl.ANY)
    dma = pltpu.SemaphoreType.DMA
    shapes = (
        jax.ShapeDtypeStruct((rows, columns), bf16),
        jax.ShapeDtypeStruct((rows // 8, KVHEADS * HEAD), bf16),
        jax.ShapeDtypeStruct((rows // 8, KVHEADS * HEAD), bf16),
        jax.ShapeDtypeStruct((TOPK, tokens), f32),
        jax.ShapeDtypeStruct((slots, hidden), bf16),
        jax.ShapeDtypeStruct((slots, hidden), bf16),
    )
    results = pl.pallas_call(
        body,
        out_shape=shapes,
        in_specs=[hbm] * 5 + [vmem] * 2 + [hbm] * 3,
        out_specs=(hbm,) * 6,
        scratch_shapes=[
            pltpu.VMEM((2, 8, 2, rows, HEAD), bf16),
            pltpu.VMEM((2, 2, width, HEAD), bf16),
            pltpu.VMEM((2, width, HEAD), bf16),
            pltpu.VMEM((18, rows, width), bf16),
            pltpu.VMEM((18, rows, width), f32),
            pltpu.VMEM((9, 8, width), f32),
            pltpu.VMEM((2, 8, width), f32),
            pltpu.VMEM((2, HEAD, width), f32),
            pltpu.VMEM((2, 8, 2, rows, HEAD), f32),
            pltpu.VMEM((2, width, HEAD), bf16),
            pltpu.VMEM((8, 2, rows, HEAD), bf16),
            pltpu.VMEM((8, 2, sub, HEAD), bf16),
            pltpu.VMEM((7, 2, sub, HEAD), bf16),
            pltpu.VMEM((7, 2, sub, HEAD), bf16),
            pltpu.VMEM((2, sub, HEAD), f32),
            pltpu.VMEM((4, rows // 8, HEAD), f32),
            pltpu.VMEM((4, rows // 8, HEAD), f32),
            pltpu.VMEM((tokens, model), bf16),
            pltpu.VMEM((slots, model + HEAD), bf16),
            pltpu.VMEM((slots, model + HEAD), bf16),
            pltpu.VMEM((slots, tokens), f32),
            pltpu.VMEM((slots, HEAD), f32),
            pltpu.VMEM((slots, HEAD), f32),
            pltpu.VMEM((slots, hidden), bf16),
            pltpu.VMEM((slots, hidden), bf16),
            pltpu.VMEM((slots, hidden), bf16),
            pltpu.VMEM((slots, hidden), bf16),
            pltpu.VMEM((rows // 8, KVHEADS * HEAD), bf16),
            pltpu.VMEM((rows // 8, KVHEADS * HEAD), bf16),
            pltpu.VMEM((TOPK, tokens), f32),
            pltpu.VMEM((2, 256, model), bf16),
            dma((2,)),
            dma((21,)),
            dma((9,)),
            dma((2, 7)),
            dma((2, 8, 2)),
            dma((2, 8, 2)),
            dma((2, 8)),
            dma((2, 2, 2)),
            dma((2, columns // HEAD)),
            dma((2, 8)),
            dma((2, 8, 2)),
            dma((2, 7)),
            dma((2, 4)),
            dma((2, 4)),
            dma((2, 7)),
        ],
        compiler_params=pltpu.CompilerParams(
            collective_id=0, has_side_effects=True, vmem_limit_bytes=61 * 1024 * 1024
        ),
    )(
        queries,
        keys,
        values,
        out_grad,
        moe_grad,
        expert_ids.T,
        gate_weights.T,
        saved_gate,
        saved_up,
        down_weight,
    )
    results = pl.pallas_call(
        hand_on,
        out_shape=shapes,
        in_specs=[vmem] * 6,
        out_specs=(vmem,) * 6,
    )(*results)
    return results[0], results[1], results[2], results[3].T, results[4], results[5]


def solution(mesh):
    both = ("ctx", "exp")
    in_specs = (
        P("ctx", "exp"),
        P("ctx", None),
        P("ctx", None),
        P("ctx", "exp"),
        P(both, None),
        P(both, None),
        P(both, None),
        P(both, None),
        P(both, None),
        P("exp", None, None),
    )
    out_specs = (
        P("ctx", "exp"),
        P(both, None),
        P(both, None),
        P(both, None),
        P(both, None),
        P(both, None),
    )
    return jax.shard_map(shards, mesh=mesh, in_specs=in_specs, out_specs=out_specs, check_vma=False)
```

```python
import jax
import jax.numpy as jnp
from jax import lax
from jax.experimental import pallas as pl
from jax.experimental.pallas import tpu as pltpu
from jax.sharding import PartitionSpec as P

KVHEADS = 2
HEAD = 128
TOPK = 8
CAP = 16
LOG2E = 1.4426950408889634
SCALE = HEAD ** (-0.5)
MESH = pl.DeviceIdType.MESH
NT = (((1,), (1,)), ((), ()))
TN = (((0,), (0,)), ((), ()))
NN = (((1,), (0,)), ((), ()))


def dot(a, b, dims):
    return lax.dot_general(a, b, dims, preferred_element_type=jnp.float32)


def flip(a, b):
    return a + b - 2 * a * b


def body(
    q_ref,
    k_ref,
    v_ref,
    do_ref,
    moe_ref,
    ids_ref,
    gw_ref,
    sg_ref,
    su_ref,
    w_ref,
    dq_ref,
    dk_ref,
    dv_ref,
    gg_ref,
    gp_ref,
    up_ref,
    kv,
    qd,
    qd_send,
    probs,
    dprob,
    maxes,
    stats,
    dq_acc,
    dkv,
    dqs,
    merge_recv,
    e1_recv,
    e2_send,
    e2_recv,
    total,
    ebk,
    ebv,
    moe,
    send_rows,
    recv_rows,
    onehot,
    score_send,
    score_recv,
    sg,
    su,
    gp,
    up,
    dk_out,
    dv_out,
    gg_out,
    w_buf,
    w_sem,
    in_sem,
    out_sem,
    a_sem,
    s1_sem,
    s2_sem,
    relay_sem,
    c_sem,
    d_sem,
    merge_sem,
    e1_sem,
    e2_sem,
    ebk_sem,
    ebv_sem,
    score_sem,
):
    c = lax.axis_index("ctx")
    e = lax.axis_index("exp")
    rows = k_ref.shape[0]
    sub = rows // 2
    heads = q_ref.shape[1] // HEAD
    width = heads * sub
    tokens, model = moe_ref.shape
    slots, hidden = sg_ref.shape
    z_hi, x, core = c // 8, (c // 2) % 4, c % 2
    chip = c // 2
    y, z_lo = e // 2, e % 2
    y_half = y % 2
    kv_head = e // 4

    def far_z(t):
        return t // 4

    def shift(t):
        m = t % 4
        return m + m // 2 - 2 * (m // 3)

    def from_chip(t):
        return flip(z_hi, far_z(t)) * 4 + (x + 4 - shift(t)) % 4

    def to_chip(t):
        return flip(z_hi, far_z(t)) * 4 + (x + shift(t)) % 4

    def to_device(t):
        return (to_chip(t) * 2 + core, y * 2 + flip(z_lo, far_z(t)))

    other_core = (c + 1 - 2 * core, e)
    partner = (15 - c, y * 2 + 1 - z_lo)
    z_mate = (c, y * 2 + 1 - z_lo)
    y_mate = (c, (y + 1 - 2 * y_half) * 2 + z_lo)

    def remote(src, dst, send_sem, recv_sem, device):
        return pltpu.make_async_remote_copy(
            src_ref=src,
            dst_ref=dst,
            send_sem=send_sem,
            recv_sem=recv_sem,
            device_id=device,
            device_id_type=MESH,
        )

    def half(index):
        return pl.ds(pl.multiple_of(index * sub, sub), sub)

    barrier = pltpu.get_barrier_semaphore()
    peers = [to_device(t) for t in range(1, 5)]
    peers += [(c, (e + step) % 8) for step in range(1, 8)]
    peers += [other_core, partner]
    for peer in peers:
        pl.semaphore_signal(barrier, inc=1, device_id=peer, device_id_type=MESH)

    head_cols = pl.ds(pl.multiple_of(kv_head * HEAD, HEAD), HEAD)
    pairs = [
        (k_ref.at[:, head_cols], kv.at[core, chip, 0]),
        (v_ref.at[:, head_cols], kv.at[core, chip, 1]),
    ]
    for n, ref in enumerate((q_ref, do_ref)):
        for h in range(heads):
            cols = pl.ds(h * HEAD, HEAD)
            pairs.append((ref.at[pl.ds(sub, sub), cols], qd_send.at[n, pl.ds(h * sub, sub), :]))
    for n, ref in enumerate((q_ref, do_ref)):
        for h in range(heads):
            cols = pl.ds(h * HEAD, HEAD)
            pairs.append((ref.at[pl.ds(0, sub), cols], qd.at[0, n, pl.ds(h * sub, sub), :]))
    pairs += [(moe_ref, moe), (sg_ref, sg), (su_ref, su)]
    loads = [
        pltpu.make_async_copy(src, dst, in_sem.at[n]) for n, (src, dst) in enumerate(pairs)
    ]
    for load in loads[: 2 + 2 * heads]:
        load.start()
    loads[2 + 4 * heads].start()

    chunk = w_buf.shape[1]
    chunks = hidden // chunk

    def weight_copy(i, slot):
        return pltpu.make_async_copy(
            w_ref.at[0, pl.ds(pl.multiple_of(i * chunk, chunk), chunk), :],
            w_buf.at[slot],
            w_sem.at[slot],
        )

    dkv[...] = jnp.zeros_like(dkv)
    dq_acc[...] = jnp.zeros_like(dq_acc)
    for s in range(2):
        stats[s, 0:1, :] = jnp.full((1, width), -1e30, jnp.float32)
        stats[s, 1:3, :] = jnp.zeros((2, width), jnp.float32)

    for load in loads[: 2 + 2 * heads]:
        load.wait()
    pl.semaphore_wait(barrier, len(peers))

    wide = width // 2

    def exchange(part, n):
        piece = pl.ds(part * wide, wide)
        return remote(
            qd_send.at[n, piece, :],
            qd.at[1, n, piece, :],
            c_sem.at[0, part, n],
            c_sem.at[1, part, n],
            partner,
        )


    def first_hop(t, n):
        if isinstance(t, int) and t > 4:
            block, index = from_chip(4), 1 - z_lo if n == 0 else y_half
            device = ((chip - x + (x + shift(t)) % 4) * 2 + core, e)
        else:
            block, index = chip, z_lo if n == 0 else y_half
            device = to_device(t)
        piece = kv.at[core, block, n, half(index), :]
        return remote(piece, piece, s1_sem.at[0, t, n], s1_sem.at[1, t, n], device)

    def second_hop(t, n):
        index = flip(z_lo, far_z(t)) if n == 0 else y_half
        piece = kv.at[core, from_chip(t), n, half(index), :]
        mate = z_mate if n == 0 else y_mate
        return remote(piece, piece, s2_sem.at[0, t, n], s2_sem.at[1, t, n], mate)

    def relay(t):
        block = kv.at[core, from_chip(t)]
        return remote(block, block, relay_sem.at[0, t], relay_sem.at[1, t], other_core)

    for n in range(2):
        first_hop(4, n).start()
    for t in range(1, 4):
        for n in range(2):
            first_hop(t, n).start()
    relay(0).start()
    weight_copy(0, 0).start()
    weight_copy(1, 1).start()
    for load in loads[2 + 2 * heads : 2 + 4 * heads] + loads[3 + 4 * heads :]:
        load.start()

    slot_row = lax.broadcasted_iota(jnp.int32, (slots, tokens), 0)
    slot_expert = slot_row // CAP
    ids = ids_ref[...]
    def route():
        weights = gw_ref[...].astype(jnp.float32)
        match = jnp.zeros((slots, tokens), jnp.float32)
        weight_of = jnp.zeros((slots, tokens), jnp.float32)
        for k in range(TOPK):
            hit = ids[k : k + 1, :] == slot_expert
            match = jnp.where(hit, 1.0, match)
            weight_of = jnp.where(hit, weights[k : k + 1, :], weight_of)
        row = lax.broadcasted_iota(jnp.int32, (tokens, tokens), 0)
        col = lax.broadcasted_iota(jnp.int32, (tokens, tokens), 1)
        earlier = jnp.where(row < col, 1.0, 0.0).astype(jnp.bfloat16)
        rank = dot(match.astype(jnp.bfloat16), earlier, NN)
        place = jnp.where(rank == (slot_row % CAP).astype(jnp.float32), match, 0.0)
        onehot[...] = place
        place_b = place.astype(jnp.bfloat16)
        loads[2 + 4 * heads].wait()
        step_cols = 512

        def gather_cols(i, carry):
            cols = pl.ds(pl.multiple_of(i * step_cols, step_cols), step_cols)
            send_rows[:, cols] = dot(place_b, moe[:, cols], NN).astype(jnp.bfloat16)
            return carry

        lax.fori_loop(0, model // step_cols, gather_cols, 0)
        slot_weight = dot(
            (place * weight_of).astype(jnp.bfloat16), jnp.ones((tokens, HEAD), jnp.bfloat16), NN
        )
        send_rows[:, model : model + HEAD] = slot_weight.astype(jnp.bfloat16)
    own_rows = pl.ds(pl.multiple_of(e * CAP, CAP), CAP)

    def far_rows(far):
        return pl.ds(pl.multiple_of(far * CAP, CAP), CAP)

    a_copies = []
    for step in range(1, 8):
        far = (e + step) % 8
        copy = remote(
            send_rows.at[far_rows(far), :],
            recv_rows.at[own_rows, :],
            a_sem.at[0, step - 1],
            a_sem.at[1, step - 1],
            (c, far),
        )
        a_copies.append(copy)

    def sub_of(s):
        return 2 * c + s * (31 - 4 * c)

    def last_of(s):
        return c + s * (15 - 2 * c)

    def last_pair(s):
        return last_of(s) // 2

    def first(s, block, cols, masked):
        place_at = 2 * (s * (c // 2 + 1) + block)
        m, l, d = stats[s, 0:1, cols], stats[s, 1:2, cols], stats[s, 2:3, cols]
        count = cols.stop - cols.start
        new = m
        scores, dprobs = [], []
        for p in range(2):
            sc = dot(kv[p, block, 0], qd[s, 0, cols, :], NT) * (SCALE * LOG2E)
            if masked:
                key_at = lax.broadcasted_iota(jnp.int32, (rows, count), 0)
                query_at = lax.broadcasted_iota(jnp.int32, (rows, count), 1) % sub
                offset = sub_of(s) * sub - (2 * block + p) * rows
                sc = jnp.where(key_at - query_at <= offset, sc, -jnp.inf)
            scores.append(sc)
            dprobs.append(dot(kv[p, block, 1], qd[s, 1, cols, :], NT))
            new = jnp.maximum(new, jnp.max(sc, axis=0, keepdims=True))
        factor = jnp.exp2(m - new)
        l = l * factor
        d = d * factor
        for p in range(2):
            ex = jnp.exp2(scores[p] - new)
            l = l + jnp.sum(ex, axis=0, keepdims=True)
            d = d + jnp.sum(ex * dprobs[p], axis=0, keepdims=True)
            probs[place_at + p, :, cols] = ex.astype(probs.dtype)
            dprob[place_at + p, :, cols] = dprobs[p]
        stats[s, 0:1, cols] = new
        stats[s, 1:2, cols] = l
        stats[s, 2:3, cols] = d
        maxes[s * (c // 2 + 1) + block, :, cols] = jnp.broadcast_to(new, (8, count))

    def first_pair(s, block, cols):
        @pl.when(block < last_pair(s))
        def _():
            first(s, block, cols, False)

        @pl.when(block == last_pair(s))
        def _():
            first(s, block, cols, True)

    def second(s, block):
        pair = s * (c // 2 + 1) + block
        scale = jnp.exp2(maxes[pair][0:1] - stats[s, 0:1, :]) * stats[s, 1:2, :]
        delta = stats[s, 2:3, :]
        dq = dq_acc[s]
        for p in range(2):
            pr = probs[2 * pair + p].astype(jnp.float32) * scale
            ds = pr * (dprob[2 * pair + p] - delta)
            p_b = pr.astype(jnp.bfloat16)
            ds_b = ds.astype(jnp.bfloat16)
            dkv[p, block, 0] += dot(ds_b, qd[s, 0], NN)
            dkv[p, block, 1] += dot(p_b, qd[s, 1], NN)
            dq = dq + dot(kv[p, block, 0], ds_b, TN)
        dq_acc[s] = dq

    def arrive(t):
        for n in range(2):
            first_hop(t, n).wait_recv()
            second_hop(t, n).start()

    def complete(t):
        for n in range(2):
            second_hop(t, n).wait_recv()
        relay(t).start()

    arrive(4)
    for t in range(5, 8):
        for n in range(2):
            first_hop(t, n).start()
    arrive(1)
    arrive(2)
    for part in range(2):
        for n in range(2):
            exchange(part, n).start()
    arrive(3)

    for load in loads[2 + 2 * heads : 2 + 4 * heads] + loads[3 + 4 * heads :]:
        load.wait()

    def first_step(i, carry):
        far = i // 8
        t = i % 4 + far * (4 + (i % 8) // 2 - i % 4)
        s = (i // 4) % 2 + far * (i % 2 - (i // 4) % 2)
        block = from_chip(t)

        @pl.when((i >= 1) & (i < 4))
        def _():
            arrive(i + 4)

        @pl.when(i < 7)
        def _():
            complete(i + 1)

        @pl.when((i < 4) | ((i >= 8) & (i % 2 == 0)))
        def _():
            relay(t).wait_recv()

        @pl.when(i == 4)
        def _():
            route()
            recv_rows[own_rows, :] = send_rows[own_rows, :]
            for copy in a_copies:
                copy.start()
            for n in range(2):
                exchange(0, n).wait()

        @pl.when(s == 0)
        def _():
            first_pair(0, block, slice(0, width))

        @pl.when(s == 1)
        def _():
            first_pair(1, block, slice(0, wide))

        return carry

    lax.fori_loop(0, 16, first_step, 0)
    for n in range(2):
        exchange(1, n).wait()

    def first_rest(t, carry):
        first_pair(1, t, slice(wide, width))
        return carry

    lax.fori_loop(0, 8, first_rest, 0)
    relay(0).wait_send()
    for t in range(1, 8):
        for n in range(2):
            first_hop(t, n).wait_send()
            second_hop(t, n).wait_send()
        relay(t).wait_send()

    for s in range(2):
        inverse = 1.0 / stats[s, 1:2, :]
        stats[s, 1:2, :] = inverse
        stats[s, 2:3, :] = stats[s, 2:3, :] * inverse

    far_core = 1 - core

    def merge(t):
        return remote(
            kv.at[far_core, to_chip(7 - t)],
            merge_recv.at[t],
            merge_sem.at[0, t],
            merge_sem.at[1, t],
            other_core,
        )

    def kept(t, n):
        return flip(z_lo, far_z(7 - t)) if n == 0 else y_half

    def mate_copy(t, n):
        return remote(
            kv.at[core, to_chip(7 - t), n, half(1 - kept(t, n)), :],
            e1_recv.at[t, n],
            e1_sem.at[0, t, n],
            e1_sem.at[1, t, n],
            z_mate if n == 0 else y_mate,
        )

    def ctx_copy(t):
        if isinstance(t, int) and t == 3:
            device = to_device(4)
        else:
            device = ((z_hi * 4 + (x + shift(7 - t)) % 4) * 2 + core, e)
        return remote(e2_send.at[t], e2_recv.at[t], e2_sem.at[0, t], e2_sem.at[1, t], device)

    def after_merge(t):
        block = to_chip(7 - t)
        merge(t).wait_recv()
        for n in range(2):
            there, here = half(1 - kept(t, n)), half(kept(t, n))
            kv[core, block, n, there, :] = (
                dkv[core, block, n, there, :] + merge_recv[t, n, there, :].astype(jnp.float32)
            ).astype(jnp.bfloat16)
            mate_copy(t, n).start()
            dkv[core, block, n, here, :] += merge_recv[t, n, here, :].astype(jnp.float32)

    def mate_sum(t, n):
        mate_copy(t, n).wait_recv()
        return dkv[core, to_chip(7 - t), n, half(kept(t, n)), :] + e1_recv[t, n].astype(
            jnp.float32
        )

    def after_mate(t):
        for n in range(2):
            e2_send[t, n] = mate_sum(t, n).astype(jnp.bfloat16)
        ctx_copy(t).start()

    def cross():
        sums = [mate_sum(3, n) for n in range(2)]
        for t in range(3):
            ctx_copy(t).wait_recv()
            for n in range(2):
                sums[n] = sums[n] + e2_recv[t, n].astype(jnp.float32)
        for n in range(2):
            e2_send[3, n] = sums[n].astype(jnp.bfloat16)
        ctx_copy(3).start()

    def second_step(t, carry):
        block = to_chip(7 - t)

        def tile(s, inner):
            @pl.when(block <= last_pair(s))
            def _():
                second(s, block)

            return inner

        lax.fori_loop(0, 2, tile, 0)
        kv[far_core, block] = dkv[far_core, block].astype(jnp.bfloat16)
        merge(t).start()

        @pl.when(t >= 2)
        def _():
            after_merge(t - 2)

        @pl.when((t >= 4) & (t < 7))
        def _():
            after_mate(t - 4)

        return carry

    lax.fori_loop(0, 8, second_step, 0)
    for s in range(1, -1, -1):
        dqs[s] = (dq_acc[s] * SCALE).T.astype(jnp.bfloat16)
        if s == 1:
            d_copies = [
                remote(
                    dqs.at[1, pl.ds(h * sub, sub), :],
                    dq_ref.at[pl.ds(sub, sub), pl.ds(h * HEAD, HEAD)],
                    d_sem.at[0, h],
                    d_sem.at[1, h],
                    partner,
                )
                for h in range(heads)
            ]
            for copy in d_copies:
                copy.start()
    after_merge(6)
    after_mate(4)
    outs = []

    def store(src, dst):
        copy = pltpu.make_async_copy(src, dst, out_sem.at[len(outs)])
        copy.start()
        outs.append(copy)

    for h in range(heads):
        store(
            dqs.at[0, pl.ds(h * sub, sub), :], dq_ref.at[pl.ds(0, sub), pl.ds(h * HEAD, HEAD)]
        )

    for copy in a_copies:
        copy.wait()
    weight_col = recv_rows[:, model : model + HEAD].astype(jnp.float32)
    weight_wide = jnp.concatenate([weight_col] * (chunk // HEAD), axis=1)

    def expert_step(i, score):
        slot = i % 2
        weight_copy(i, slot).wait()
        cols = pl.ds(pl.multiple_of(i * chunk, chunk), chunk)
        back = dot(recv_rows[:, 0:model], w_buf[slot], NT)

        @pl.when(i + 2 < chunks)
        def _():
            weight_copy(i + 2, slot).start()

        g = sg[:, cols].astype(jnp.float32)
        u = su[:, cols].astype(jnp.float32)
        sig = 1.0 / (1.0 + jnp.exp(-g))
        silu = g * sig
        act = (silu * u).astype(jnp.bfloat16).astype(jnp.float32)
        act_grad = weight_wide * back
        gp[:, cols] = (act_grad * u * sig * (1.0 + g * (1.0 - sig))).astype(jnp.bfloat16)
        up[:, cols] = (act_grad * silu).astype(jnp.bfloat16)
        return score + jnp.sum(act * back, axis=1, keepdims=True)

    after_merge(7)
    score = lax.fori_loop(0, 2, expert_step, jnp.zeros((slots, 1), jnp.float32))
    cross()
    after_mate(5)
    score = lax.fori_loop(2, 4, expert_step, score)
    after_mate(6)
    score = lax.fori_loop(4, chunks, expert_step, score)
    score_send[...] = jnp.broadcast_to(score, (slots, HEAD))
    score_copies = []
    for step in range(1, 8):
        far = (e + step) % 8
        copy = remote(
            score_send.at[far_rows(far), :],
            score_recv.at[own_rows, :],
            score_sem.at[0, step - 1],
            score_sem.at[1, step - 1],
            (c, far),
        )
        copy.start()
        score_copies.append(copy)
    score_recv[own_rows, :] = score_send[own_rows, :]
    store(gp, gp_ref)
    store(up, up_ref)

    for n in range(2):
        total[n] = mate_sum(7, n)
    for t in range(3, 7):
        ctx_copy(t).wait_recv()
        total[...] += e2_recv[t].astype(jnp.float32)
    part = rows // 8

    def owner_copy(n, i):
        rows_i = pl.ds(i * part, part)
        if n == 0:
            return remote(
                total.at[0, rows_i, :], ebk.at[y], ebk_sem.at[0, i], ebk_sem.at[1, y], (c, 4 * z_lo + i)
            )
        source = (y // 2) * 2 + z_lo
        return remote(
            total.at[1, rows_i, :],
            ebv.at[source],
            ebv_sem.at[0, i],
            ebv_sem.at[1, source],
            (c, 4 * y_half + i),
        )

    def owner_of(n, i):
        return 4 * (z_lo if n == 0 else y_half) + i

    for n in range(2):
        for i in range(4):

            @pl.when(owner_of(n, i) != e)
            def _():
                owner_copy(n, i).start()

            @pl.when(owner_of(n, i) == e)
            def _():
                if n == 0:
                    ebk[y] = total[0, i * part : (i + 1) * part, :]
                else:
                    ebv[(y // 2) * 2 + z_lo] = total[1, i * part : (i + 1) * part, :]

    for copy in score_copies:
        copy.wait()
    picked = onehot[...] * score_recv[...]
    for k in range(TOPK):
        gg_out[k : k + 1, :] = jnp.sum(
            jnp.where(ids[k : k + 1, :] == slot_expert, picked, 0.0), axis=0, keepdims=True
        )
    store(gg_out, gg_ref)

    for i in range(4):
        source_k = 2 * i + e // 4
        source_v = (2 * (i // 2) + e // 4) * 2 + i % 2

        @pl.when(source_k != e)
        def _():
            remote(ebk.at[i], ebk.at[i], ebk_sem.at[0, i], ebk_sem.at[1, i], other_core).wait_recv()

        @pl.when(source_v != e)
        def _():
            remote(ebv.at[i], ebv.at[i], ebv_sem.at[0, i], ebv_sem.at[1, i], other_core).wait_recv()

    for kv_index in range(KVHEADS):
        cols = slice(kv_index * HEAD, (kv_index + 1) * HEAD)
        first_source = 2 * kv_index
        dk_out[:, cols] = ((ebk[first_source] + ebk[first_source + 1]) * SCALE).astype(jnp.bfloat16)
        dv_out[:, cols] = (ebv[first_source] + ebv[first_source + 1]).astype(jnp.bfloat16)
    store(dk_out, dk_ref)
    store(dv_out, dv_ref)

    for t in range(8):
        merge(t).wait_send()
        for n in range(2):
            mate_copy(t, n).wait_send()
        if t < 7:
            ctx_copy(t).wait_send()
    for n in range(2):
        for i in range(4):

            @pl.when(owner_of(n, i) != e)
            def _():
                owner_copy(n, i).wait_send()

    for copy in d_copies + outs:
        copy.wait()


def hand_on(*refs):
    count = len(refs) // 2
    for n in range(count):
        refs[count + n][...] = refs[n][...]


def shards(
    queries,
    keys,
    values,
    out_grad,
    moe_grad,
    expert_ids,
    gate_weights,
    saved_gate,
    saved_up,
    down_weight,
):
    rows, columns = queries.shape
    sub = rows // 2
    width = columns // HEAD * sub
    tokens, model = moe_grad.shape
    slots, hidden = saved_gate.shape
    bf16, f32 = jnp.bfloat16, jnp.float32
    vmem = pl.BlockSpec(memory_space=pltpu.VMEM)
    hbm = pl.BlockSpec(memory_space=pl.ANY)
    dma = pltpu.SemaphoreType.DMA
    shapes = (
        jax.ShapeDtypeStruct((rows, columns), bf16),
        jax.ShapeDtypeStruct((rows // 8, KVHEADS * HEAD), bf16),
        jax.ShapeDtypeStruct((rows // 8, KVHEADS * HEAD), bf16),
        jax.ShapeDtypeStruct((TOPK, tokens), f32),
        jax.ShapeDtypeStruct((slots, hidden), bf16),
        jax.ShapeDtypeStruct((slots, hidden), bf16),
    )
    results = pl.pallas_call(
        body,
        out_shape=shapes,
        in_specs=[hbm] * 5 + [vmem] * 2 + [hbm] * 3,
        out_specs=(hbm,) * 6,
        scratch_shapes=[
            pltpu.VMEM((2, 8, 2, rows, HEAD), bf16),
            pltpu.VMEM((2, 2, width, HEAD), bf16),
            pltpu.VMEM((2, width, HEAD), bf16),
            pltpu.VMEM((18, rows, width), bf16),
            pltpu.VMEM((18, rows, width), f32),
            pltpu.VMEM((9, 8, width), f32),
            pltpu.VMEM((2, 8, width), f32),
            pltpu.VMEM((2, HEAD, width), f32),
            pltpu.VMEM((2, 8, 2, rows, HEAD), f32),
            pltpu.VMEM((2, width, HEAD), bf16),
            pltpu.VMEM((8, 2, rows, HEAD), bf16),
            pltpu.VMEM((8, 2, sub, HEAD), bf16),
            pltpu.VMEM((7, 2, sub, HEAD), bf16),
            pltpu.VMEM((7, 2, sub, HEAD), bf16),
            pltpu.VMEM((2, sub, HEAD), f32),
            pltpu.VMEM((4, rows // 8, HEAD), f32),
            pltpu.VMEM((4, rows // 8, HEAD), f32),
            pltpu.VMEM((tokens, model), bf16),
            pltpu.VMEM((slots, model + HEAD), bf16),
            pltpu.VMEM((slots, model + HEAD), bf16),
            pltpu.VMEM((slots, tokens), f32),
            pltpu.VMEM((slots, HEAD), f32),
            pltpu.VMEM((slots, HEAD), f32),
            pltpu.VMEM((slots, hidden), bf16),
            pltpu.VMEM((slots, hidden), bf16),
            pltpu.VMEM((slots, hidden), bf16),
            pltpu.VMEM((slots, hidden), bf16),
            pltpu.VMEM((rows // 8, KVHEADS * HEAD), bf16),
            pltpu.VMEM((rows // 8, KVHEADS * HEAD), bf16),
            pltpu.VMEM((TOPK, tokens), f32),
            pltpu.VMEM((2, 256, model), bf16),
            dma((2,)),
            dma((21,)),
            dma((9,)),
            dma((2, 7)),
            dma((2, 8, 2)),
            dma((2, 8, 2)),
            dma((2, 8)),
            dma((2, 2, 2)),
            dma((2, columns // HEAD)),
            dma((2, 8)),
            dma((2, 8, 2)),
            dma((2, 7)),
            dma((2, 4)),
            dma((2, 4)),
            dma((2, 7)),
        ],
        compiler_params=pltpu.CompilerParams(
            collective_id=0, has_side_effects=True, vmem_limit_bytes=61 * 1024 * 1024
        ),
    )(
        queries,
        keys,
        values,
        out_grad,
        moe_grad,
        expert_ids.T,
        gate_weights.T,
        saved_gate,
        saved_up,
        down_weight,
    )
    results = pl.pallas_call(
        hand_on,
        out_shape=shapes,
        in_specs=[vmem] * 6,
        out_specs=(vmem,) * 6,
    )(*results)
    return results[0], results[1], results[2], results[3].T, results[4], results[5]


def solution(mesh):
    both = ("ctx", "exp")
    in_specs = (
        P("ctx", "exp"),
        P("ctx", None),
        P("ctx", None),
        P("ctx", "exp"),
        P(both, None),
        P(both, None),
        P(both, None),
        P(both, None),
        P(both, None),
        P("exp", None, None),
    )
    out_specs = (
        P("ctx", "exp"),
        P(both, None),
        P(both, None),
        P(both, None),
        P(both, None),
        P(both, None),
    )
    return jax.shard_map(shards, mesh=mesh, in_specs=in_specs, out_specs=out_specs, check_vma=False)
```

```python
import jax
import jax.numpy as jnp
from jax import lax
from jax.experimental import pallas as pl
from jax.experimental.pallas import tpu as pltpu
from jax.sharding import PartitionSpec as P

KVHEADS = 2
HEAD = 128
TOPK = 8
CAP = 16
LOG2E = 1.4426950408889634
SCALE = HEAD ** (-0.5)
MESH = pl.DeviceIdType.MESH
NT = (((1,), (1,)), ((), ()))
TN = (((0,), (0,)), ((), ()))
NN = (((1,), (0,)), ((), ()))


def dot(a, b, dims):
    return lax.dot_general(a, b, dims, preferred_element_type=jnp.float32)


def flip(a, b):
    return a + b - 2 * a * b


def body(
    q_ref,
    k_ref,
    v_ref,
    do_ref,
    moe_ref,
    ids_ref,
    gw_ref,
    sg_ref,
    su_ref,
    w_ref,
    dq_ref,
    dk_ref,
    dv_ref,
    gg_ref,
    gp_ref,
    up_ref,
    kv,
    qd,
    qd_send,
    probs,
    dprob,
    maxes,
    stats,
    dq_acc,
    dkv,
    dqs,
    merge_recv,
    e1_recv,
    e2_send,
    e2_recv,
    total,
    ebk,
    ebv,
    moe,
    send_rows,
    recv_rows,
    onehot,
    score_send,
    score_recv,
    sg,
    su,
    gp,
    up,
    dk_out,
    dv_out,
    gg_out,
    w_buf,
    w_sem,
    in_sem,
    out_sem,
    a_sem,
    s1_sem,
    s2_sem,
    relay_sem,
    c_sem,
    d_sem,
    merge_sem,
    e1_sem,
    e2_sem,
    ebk_sem,
    ebv_sem,
    score_sem,
):
    c = lax.axis_index("ctx")
    e = lax.axis_index("exp")
    rows = k_ref.shape[0]
    sub = rows // 2
    heads = q_ref.shape[1] // HEAD
    width = heads * sub
    tokens, model = moe_ref.shape
    slots, hidden = sg_ref.shape
    z_hi, x, core = c // 8, (c // 2) % 4, c % 2
    chip = c // 2
    y, z_lo = e // 2, e % 2
    y_half = y % 2
    kv_head = e // 4

    def far_z(t):
        return t // 4

    def shift(t):
        m = t % 4
        return m + m // 2 - 2 * (m // 3)

    def from_chip(t):
        return flip(z_hi, far_z(t)) * 4 + (x + 4 - shift(t)) % 4

    def to_chip(t):
        return flip(z_hi, far_z(t)) * 4 + (x + shift(t)) % 4

    def to_device(t):
        return (to_chip(t) * 2 + core, y * 2 + flip(z_lo, far_z(t)))

    other_core = (c + 1 - 2 * core, e)
    partner = (15 - c, y * 2 + 1 - z_lo)
    z_mate = (c, y * 2 + 1 - z_lo)
    y_mate = (c, (y + 1 - 2 * y_half) * 2 + z_lo)

    def remote(src, dst, send_sem, recv_sem, device):
        return pltpu.make_async_remote_copy(
            src_ref=src,
            dst_ref=dst,
            send_sem=send_sem,
            recv_sem=recv_sem,
            device_id=device,
            device_id_type=MESH,
        )

    def half(index):
        return pl.ds(pl.multiple_of(index * sub, sub), sub)

    barrier = pltpu.get_barrier_semaphore()
    peers = [to_device(t) for t in range(1, 5)]
    peers += [(c, (e + step) % 8) for step in range(1, 8)]
    peers += [other_core, partner]
    for peer in peers:
        pl.semaphore_signal(barrier, inc=1, device_id=peer, device_id_type=MESH)

    head_cols = pl.ds(pl.multiple_of(kv_head * HEAD, HEAD), HEAD)
    pairs = [
        (k_ref.at[:, head_cols], kv.at[core, chip, 0]),
        (v_ref.at[:, head_cols], kv.at[core, chip, 1]),
    ]
    for n, ref in enumerate((q_ref, do_ref)):
        for h in range(heads):
            cols = pl.ds(h * HEAD, HEAD)
            pairs.append((ref.at[pl.ds(sub, sub), cols], qd_send.at[n, pl.ds(h * sub, sub), :]))
    for n, ref in enumerate((q_ref, do_ref)):
        for h in range(heads):
            cols = pl.ds(h * HEAD, HEAD)
            pairs.append((ref.at[pl.ds(0, sub), cols], qd.at[0, n, pl.ds(h * sub, sub), :]))
    pairs += [(moe_ref, moe), (sg_ref, sg), (su_ref, su)]
    loads = [
        pltpu.make_async_copy(src, dst, in_sem.at[n]) for n, (src, dst) in enumerate(pairs)
    ]
    for load in loads[: 2 + 2 * heads]:
        load.start()
    loads[2 + 4 * heads].start()

    chunk = w_buf.shape[1]
    chunks = hidden // chunk

    def weight_copy(i, slot):
        return pltpu.make_async_copy(
            w_ref.at[0, pl.ds(pl.multiple_of(i * chunk, chunk), chunk), :],
            w_buf.at[slot],
            w_sem.at[slot],
        )

    dkv[...] = jnp.zeros_like(dkv)
    dq_acc[...] = jnp.zeros_like(dq_acc)
    for s in range(2):
        stats[s, 0:1, :] = jnp.full((1, width), -1e30, jnp.float32)
        stats[s, 1:3, :] = jnp.zeros((2, width), jnp.float32)

    for load in loads[: 2 + 2 * heads]:
        load.wait()
    pl.semaphore_wait(barrier, len(peers))

    wide = width // 2

    def exchange(part, n):
        piece = pl.ds(part * wide, wide)
        return remote(
            qd_send.at[n, piece, :],
            qd.at[1, n, piece, :],
            c_sem.at[0, part, n],
            c_sem.at[1, part, n],
            partner,
        )


    def first_hop(t, n):
        if isinstance(t, int) and t > 4:
            block, index = from_chip(4), 1 - z_lo if n == 0 else y_half
            device = ((chip - x + (x + shift(t)) % 4) * 2 + core, e)
        else:
            block, index = chip, z_lo if n == 0 else y_half
            device = to_device(t)
        piece = kv.at[core, block, n, half(index), :]
        return remote(piece, piece, s1_sem.at[0, t, n], s1_sem.at[1, t, n], device)

    def second_hop(t, n):
        index = flip(z_lo, far_z(t)) if n == 0 else y_half
        piece = kv.at[core, from_chip(t), n, half(index), :]
        mate = z_mate if n == 0 else y_mate
        return remote(piece, piece, s2_sem.at[0, t, n], s2_sem.at[1, t, n], mate)

    def relay(t):
        block = kv.at[core, from_chip(t)]
        return remote(block, block, relay_sem.at[0, t], relay_sem.at[1, t], other_core)

    for n in range(2):
        first_hop(4, n).start()
    for t in range(1, 4):
        for n in range(2):
            first_hop(t, n).start()
    relay(0).start()
    weight_copy(0, 0).start()
    weight_copy(1, 1).start()
    for load in loads[2 + 2 * heads : 2 + 4 * heads] + loads[3 + 4 * heads :]:
        load.start()

    slot_row = lax.broadcasted_iota(jnp.int32, (slots, tokens), 0)
    slot_expert = slot_row // CAP
    ids = ids_ref[...]
    def route():
        weights = gw_ref[...].astype(jnp.float32)
        match = jnp.zeros((slots, tokens), jnp.float32)
        weight_of = jnp.zeros((slots, tokens), jnp.float32)
        for k in range(TOPK):
            hit = ids[k : k + 1, :] == slot_expert
            match = jnp.where(hit, 1.0, match)
            weight_of = jnp.where(hit, weights[k : k + 1, :], weight_of)
        row = lax.broadcasted_iota(jnp.int32, (tokens, tokens), 0)
        col = lax.broadcasted_iota(jnp.int32, (tokens, tokens), 1)
        earlier = jnp.where(row < col, 1.0, 0.0).astype(jnp.bfloat16)
        rank = dot(match.astype(jnp.bfloat16), earlier, NN)
        place = jnp.where(rank == (slot_row % CAP).astype(jnp.float32), match, 0.0)
        onehot[...] = place
        place_b = place.astype(jnp.bfloat16)
        loads[2 + 4 * heads].wait()
        step_cols = 512

        def gather_cols(i, carry):
            cols = pl.ds(pl.multiple_of(i * step_cols, step_cols), step_cols)
            send_rows[:, cols] = dot(place_b, moe[:, cols], NN).astype(jnp.bfloat16)
            return carry

        lax.fori_loop(0, model // step_cols, gather_cols, 0)
        slot_weight = dot(
            (place * weight_of).astype(jnp.bfloat16), jnp.ones((tokens, HEAD), jnp.bfloat16), NN
        )
        send_rows[:, model : model + HEAD] = slot_weight.astype(jnp.bfloat16)
    own_rows = pl.ds(pl.multiple_of(e * CAP, CAP), CAP)

    def far_rows(far):
        return pl.ds(pl.multiple_of(far * CAP, CAP), CAP)

    a_copies = []
    for step in range(1, 8):
        far = (e + step) % 8
        copy = remote(
            send_rows.at[far_rows(far), :],
            recv_rows.at[own_rows, :],
            a_sem.at[0, step - 1],
            a_sem.at[1, step - 1],
            (c, far),
        )
        a_copies.append(copy)

    def sub_of(s):
        return 2 * c + s * (31 - 4 * c)

    def last_of(s):
        return c + s * (15 - 2 * c)

    def last_pair(s):
        return last_of(s) // 2

    def first(s, block, cols, masked):
        place_at = 2 * (s * (c // 2 + 1) + block)
        m, l, d = stats[s, 0:1, cols], stats[s, 1:2, cols], stats[s, 2:3, cols]
        count = cols.stop - cols.start
        new = m
        scores, dprobs = [], []
        for p in range(2):
            sc = dot(kv[p, block, 0], qd[s, 0, cols, :], NT) * (SCALE * LOG2E)
            if masked:
                key_at = lax.broadcasted_iota(jnp.int32, (rows, count), 0)
                query_at = lax.broadcasted_iota(jnp.int32, (rows, count), 1) % sub
                offset = sub_of(s) * sub - (2 * block + p) * rows
                sc = jnp.where(key_at - query_at <= offset, sc, -jnp.inf)
            scores.append(sc)
            dprobs.append(dot(kv[p, block, 1], qd[s, 1, cols, :], NT))
            new = jnp.maximum(new, jnp.max(sc, axis=0, keepdims=True))
        factor = jnp.exp2(m - new)
        l = l * factor
        d = d * factor
        for p in range(2):
            ex = jnp.exp2(scores[p] - new)
            l = l + jnp.sum(ex, axis=0, keepdims=True)
            d = d + jnp.sum(ex * dprobs[p], axis=0, keepdims=True)
            probs[place_at + p, :, cols] = ex.astype(probs.dtype)
            dprob[place_at + p, :, cols] = dprobs[p]
        stats[s, 0:1, cols] = new
        stats[s, 1:2, cols] = l
        stats[s, 2:3, cols] = d
        maxes[s * (c // 2 + 1) + block, :, cols] = jnp.broadcast_to(new, (8, count))

    def first_pair(s, block, cols):
        @pl.when(block < last_pair(s))
        def _():
            first(s, block, cols, False)

        @pl.when(block == last_pair(s))
        def _():
            first(s, block, cols, True)

    def second(s, block):
        pair = s * (c // 2 + 1) + block
        scale = jnp.exp2(maxes[pair][0:1] - stats[s, 0:1, :]) * stats[s, 1:2, :]
        delta = stats[s, 2:3, :]
        dq = dq_acc[s]
        for p in range(2):
            pr = probs[2 * pair + p].astype(jnp.float32) * scale
            ds = pr * (dprob[2 * pair + p] - delta)
            p_b = pr.astype(jnp.bfloat16)
            ds_b = ds.astype(jnp.bfloat16)
            dkv[p, block, 0] += dot(ds_b, qd[s, 0], NN)
            dkv[p, block, 1] += dot(p_b, qd[s, 1], NN)
            dq = dq + dot(kv[p, block, 0], ds_b, TN)
        dq_acc[s] = dq

    def arrive(t):
        for n in range(2):
            first_hop(t, n).wait_recv()
            second_hop(t, n).start()

    def complete(t):
        for n in range(2):
            second_hop(t, n).wait_recv()
        relay(t).start()

    arrive(4)
    for t in range(5, 8):
        for n in range(2):
            first_hop(t, n).start()
    arrive(1)
    arrive(2)
    for part in range(2):
        for n in range(2):
            exchange(part, n).start()
    arrive(3)

    for load in loads[2 + 2 * heads : 2 + 4 * heads] + loads[3 + 4 * heads :]:
        load.wait()

    def first_step(i, carry):
        far = i // 8
        t = i % 4 + far * (4 + (i % 8) // 2 - i % 4)
        s = (i // 4) % 2 + far * (i % 2 - (i // 4) % 2)
        block = from_chip(t)

        @pl.when((i >= 1) & (i < 4))
        def _():
            arrive(i + 4)

        @pl.when(i < 7)
        def _():
            complete(i + 1)

        @pl.when((i < 4) | ((i >= 8) & (i % 2 == 0)))
        def _():
            relay(t).wait_recv()

        @pl.when(i == 4)
        def _():
            route()
            recv_rows[own_rows, :] = send_rows[own_rows, :]
            for copy in a_copies:
                copy.start()
            for n in range(2):
                exchange(0, n).wait()

        @pl.when(s == 0)
        def _():
            first_pair(0, block, slice(0, width))

        @pl.when(s == 1)
        def _():
            first_pair(1, block, slice(0, wide))

        return carry

    lax.fori_loop(0, 16, first_step, 0)
    for n in range(2):
        exchange(1, n).wait()

    def first_rest(t, carry):
        first_pair(1, t, slice(wide, width))
        return carry

    lax.fori_loop(0, 8, first_rest, 0)
    relay(0).wait_send()
    for t in range(1, 8):
        for n in range(2):
            first_hop(t, n).wait_send()
            second_hop(t, n).wait_send()
        relay(t).wait_send()

    for s in range(2):
        inverse = 1.0 / stats[s, 1:2, :]
        stats[s, 1:2, :] = inverse
        stats[s, 2:3, :] = stats[s, 2:3, :] * inverse

    far_core = 1 - core

    def merge(t):
        return remote(
            kv.at[far_core, to_chip(7 - t)],
            merge_recv.at[t],
            merge_sem.at[0, t],
            merge_sem.at[1, t],
            other_core,
        )

    def kept(t, n):
        return flip(z_lo, far_z(7 - t)) if n == 0 else y_half

    def mate_copy(t, n):
        return remote(
            kv.at[core, to_chip(7 - t), n, half(1 - kept(t, n)), :],
            e1_recv.at[t, n],
            e1_sem.at[0, t, n],
            e1_sem.at[1, t, n],
            z_mate if n == 0 else y_mate,
        )

    def ctx_copy(t):
        if isinstance(t, int) and t == 3:
            device = to_device(4)
        else:
            device = ((z_hi * 4 + (x + shift(7 - t)) % 4) * 2 + core, e)
        return remote(e2_send.at[t], e2_recv.at[t], e2_sem.at[0, t], e2_sem.at[1, t], device)

    def after_merge(t):
        block = to_chip(7 - t)
        merge(t).wait_recv()
        for n in range(2):
            there, here = half(1 - kept(t, n)), half(kept(t, n))
            kv[core, block, n, there, :] = (
                dkv[core, block, n, there, :] + merge_recv[t, n, there, :].astype(jnp.float32)
            ).astype(jnp.bfloat16)
            mate_copy(t, n).start()
            dkv[core, block, n, here, :] += merge_recv[t, n, here, :].astype(jnp.float32)

    def mate_sum(t, n):
        mate_copy(t, n).wait_recv()
        return dkv[core, to_chip(7 - t), n, half(kept(t, n)), :] + e1_recv[t, n].astype(
            jnp.float32
        )

    def after_mate(t):
        for n in range(2):
            e2_send[t, n] = mate_sum(t, n).astype(jnp.bfloat16)
        ctx_copy(t).start()

    def cross():
        sums = [mate_sum(3, n) for n in range(2)]
        for t in range(3):
            ctx_copy(t).wait_recv()
            for n in range(2):
                sums[n] = sums[n] + e2_recv[t, n].astype(jnp.float32)
        for n in range(2):
            e2_send[3, n] = sums[n].astype(jnp.bfloat16)
        ctx_copy(3).start()

    def second_step(t, carry):
        block = to_chip(7 - t)

        def tile(s, inner):
            @pl.when(block <= last_pair(s))
            def _():
                second(s, block)

            return inner

        lax.fori_loop(0, 2, tile, 0)
        kv[far_core, block] = dkv[far_core, block].astype(jnp.bfloat16)
        merge(t).start()

        @pl.when(t >= 2)
        def _():
            after_merge(t - 2)

        @pl.when((t >= 4) & (t < 7))
        def _():
            after_mate(t - 4)

        return carry

    lax.fori_loop(0, 8, second_step, 0)
    dqs[1] = (dq_acc[1] * SCALE).T.astype(jnp.bfloat16)
    d_copies = [
        remote(
            dqs.at[1, pl.ds(h * sub, sub), :],
            dq_ref.at[pl.ds(sub, sub), pl.ds(h * HEAD, HEAD)],
            d_sem.at[0, h],
            d_sem.at[1, h],
            partner,
        )
        for h in range(heads)
    ]
    for copy in d_copies:
        copy.start()
    after_merge(6)
    after_mate(4)
    outs = []

    def store(src, dst):
        copy = pltpu.make_async_copy(src, dst, out_sem.at[len(outs)])
        copy.start()
        outs.append(copy)

    for copy in a_copies:
        copy.wait()
    weight_col = recv_rows[:, model : model + HEAD].astype(jnp.float32)
    weight_wide = jnp.concatenate([weight_col] * (chunk // HEAD), axis=1)

    def expert_step(i, score):
        slot = i % 2
        weight_copy(i, slot).wait()
        cols = pl.ds(pl.multiple_of(i * chunk, chunk), chunk)
        back = dot(recv_rows[:, 0:model], w_buf[slot], NT)

        @pl.when(i + 2 < chunks)
        def _():
            weight_copy(i + 2, slot).start()

        g = sg[:, cols].astype(jnp.float32)
        u = su[:, cols].astype(jnp.float32)
        sig = 1.0 / (1.0 + jnp.exp(-g))
        silu = g * sig
        act = (silu * u).astype(jnp.bfloat16).astype(jnp.float32)
        act_grad = weight_wide * back
        gp[:, cols] = (act_grad * u * sig * (1.0 + g * (1.0 - sig))).astype(jnp.bfloat16)
        up[:, cols] = (act_grad * silu).astype(jnp.bfloat16)
        return score + jnp.sum(act * back, axis=1, keepdims=True)

    after_merge(7)
    dqs[0] = (dq_acc[0] * SCALE).T.astype(jnp.bfloat16)
    for h in range(heads):
        store(
            dqs.at[0, pl.ds(h * sub, sub), :], dq_ref.at[pl.ds(0, sub), pl.ds(h * HEAD, HEAD)]
        )
    score = lax.fori_loop(0, 2, expert_step, jnp.zeros((slots, 1), jnp.float32))
    cross()
    after_mate(5)
    score = lax.fori_loop(2, 4, expert_step, score)
    after_mate(6)
    score = lax.fori_loop(4, chunks, expert_step, score)
    score_send[...] = jnp.broadcast_to(score, (slots, HEAD))
    score_copies = []
    for step in range(1, 8):
        far = (e + step) % 8
        copy = remote(
            score_send.at[far_rows(far), :],
            score_recv.at[own_rows, :],
            score_sem.at[0, step - 1],
            score_sem.at[1, step - 1],
            (c, far),
        )
        copy.start()
        score_copies.append(copy)
    score_recv[own_rows, :] = score_send[own_rows, :]
    store(gp, gp_ref)
    store(up, up_ref)

    for n in range(2):
        total[n] = mate_sum(7, n)
    for t in range(3, 7):
        ctx_copy(t).wait_recv()
        total[...] += e2_recv[t].astype(jnp.float32)
    part = rows // 8

    def owner_copy(n, i):
        rows_i = pl.ds(i * part, part)
        if n == 0:
            return remote(
                total.at[0, rows_i, :], ebk.at[y], ebk_sem.at[0, i], ebk_sem.at[1, y], (c, 4 * z_lo + i)
            )
        source = (y // 2) * 2 + z_lo
        return remote(
            total.at[1, rows_i, :],
            ebv.at[source],
            ebv_sem.at[0, i],
            ebv_sem.at[1, source],
            (c, 4 * y_half + i),
        )

    def owner_of(n, i):
        return 4 * (z_lo if n == 0 else y_half) + i

    for n in range(2):
        for i in range(4):

            @pl.when(owner_of(n, i) != e)
            def _():
                owner_copy(n, i).start()

            @pl.when(owner_of(n, i) == e)
            def _():
                if n == 0:
                    ebk[y] = total[0, i * part : (i + 1) * part, :]
                else:
                    ebv[(y // 2) * 2 + z_lo] = total[1, i * part : (i + 1) * part, :]

    for copy in score_copies:
        copy.wait()
    picked = onehot[...] * score_recv[...]
    for k in range(TOPK):
        gg_out[k : k + 1, :] = jnp.sum(
            jnp.where(ids[k : k + 1, :] == slot_expert, picked, 0.0), axis=0, keepdims=True
        )
    store(gg_out, gg_ref)

    for i in range(4):
        source_k = 2 * i + e // 4
        source_v = (2 * (i // 2) + e // 4) * 2 + i % 2

        @pl.when(source_k != e)
        def _():
            remote(ebk.at[i], ebk.at[i], ebk_sem.at[0, i], ebk_sem.at[1, i], other_core).wait_recv()

        @pl.when(source_v != e)
        def _():
            remote(ebv.at[i], ebv.at[i], ebv_sem.at[0, i], ebv_sem.at[1, i], other_core).wait_recv()

    for kv_index in range(KVHEADS):
        cols = slice(kv_index * HEAD, (kv_index + 1) * HEAD)
        first_source = 2 * kv_index
        dk_out[:, cols] = ((ebk[first_source] + ebk[first_source + 1]) * SCALE).astype(jnp.bfloat16)
        dv_out[:, cols] = (ebv[first_source] + ebv[first_source + 1]).astype(jnp.bfloat16)
    store(dk_out, dk_ref)
    store(dv_out, dv_ref)

    for t in range(8):
        merge(t).wait_send()
        for n in range(2):
            mate_copy(t, n).wait_send()
        if t < 7:
            ctx_copy(t).wait_send()
    for n in range(2):
        for i in range(4):

            @pl.when(owner_of(n, i) != e)
            def _():
                owner_copy(n, i).wait_send()

    for copy in d_copies + outs:
        copy.wait()


def hand_on(*refs):
    count = len(refs) // 2
    for n in range(count):
        refs[count + n][...] = refs[n][...]


def shards(
    queries,
    keys,
    values,
    out_grad,
    moe_grad,
    expert_ids,
    gate_weights,
    saved_gate,
    saved_up,
    down_weight,
):
    rows, columns = queries.shape
    sub = rows // 2
    width = columns // HEAD * sub
    tokens, model = moe_grad.shape
    slots, hidden = saved_gate.shape
    bf16, f32 = jnp.bfloat16, jnp.float32
    vmem = pl.BlockSpec(memory_space=pltpu.VMEM)
    hbm = pl.BlockSpec(memory_space=pl.ANY)
    dma = pltpu.SemaphoreType.DMA
    shapes = (
        jax.ShapeDtypeStruct((rows, columns), bf16),
        jax.ShapeDtypeStruct((rows // 8, KVHEADS * HEAD), bf16),
        jax.ShapeDtypeStruct((rows // 8, KVHEADS * HEAD), bf16),
        jax.ShapeDtypeStruct((TOPK, tokens), f32),
        jax.ShapeDtypeStruct((slots, hidden), bf16),
        jax.ShapeDtypeStruct((slots, hidden), bf16),
    )
    results = pl.pallas_call(
        body,
        out_shape=shapes,
        in_specs=[hbm] * 5 + [vmem] * 2 + [hbm] * 3,
        out_specs=(hbm,) * 6,
        scratch_shapes=[
            pltpu.VMEM((2, 8, 2, rows, HEAD), bf16),
            pltpu.VMEM((2, 2, width, HEAD), bf16),
            pltpu.VMEM((2, width, HEAD), bf16),
            pltpu.VMEM((18, rows, width), bf16),
            pltpu.VMEM((18, rows, width), f32),
            pltpu.VMEM((9, 8, width), f32),
            pltpu.VMEM((2, 8, width), f32),
            pltpu.VMEM((2, HEAD, width), f32),
            pltpu.VMEM((2, 8, 2, rows, HEAD), f32),
            pltpu.VMEM((2, width, HEAD), bf16),
            pltpu.VMEM((8, 2, rows, HEAD), bf16),
            pltpu.VMEM((8, 2, sub, HEAD), bf16),
            pltpu.VMEM((7, 2, sub, HEAD), bf16),
            pltpu.VMEM((7, 2, sub, HEAD), bf16),
            pltpu.VMEM((2, sub, HEAD), f32),
            pltpu.VMEM((4, rows // 8, HEAD), f32),
            pltpu.VMEM((4, rows // 8, HEAD), f32),
            pltpu.VMEM((tokens, model), bf16),
            pltpu.VMEM((slots, model + HEAD), bf16),
            pltpu.VMEM((slots, model + HEAD), bf16),
            pltpu.VMEM((slots, tokens), f32),
            pltpu.VMEM((slots, HEAD), f32),
            pltpu.VMEM((slots, HEAD), f32),
            pltpu.VMEM((slots, hidden), bf16),
            pltpu.VMEM((slots, hidden), bf16),
            pltpu.VMEM((slots, hidden), bf16),
            pltpu.VMEM((slots, hidden), bf16),
            pltpu.VMEM((rows // 8, KVHEADS * HEAD), bf16),
            pltpu.VMEM((rows // 8, KVHEADS * HEAD), bf16),
            pltpu.VMEM((TOPK, tokens), f32),
            pltpu.VMEM((2, 256, model), bf16),
            dma((2,)),
            dma((21,)),
            dma((9,)),
            dma((2, 7)),
            dma((2, 8, 2)),
            dma((2, 8, 2)),
            dma((2, 8)),
            dma((2, 2, 2)),
            dma((2, columns // HEAD)),
            dma((2, 8)),
            dma((2, 8, 2)),
            dma((2, 7)),
            dma((2, 4)),
            dma((2, 4)),
            dma((2, 7)),
        ],
        compiler_params=pltpu.CompilerParams(
            collective_id=0, has_side_effects=True, vmem_limit_bytes=61 * 1024 * 1024
        ),
    )(
        queries,
        keys,
        values,
        out_grad,
        moe_grad,
        expert_ids.T,
        gate_weights.T,
        saved_gate,
        saved_up,
        down_weight,
    )
    results = pl.pallas_call(
        hand_on,
        out_shape=shapes,
        in_specs=[vmem] * 6,
        out_specs=(vmem,) * 6,
    )(*results)
    return results[0], results[1], results[2], results[3].T, results[4], results[5]


def solution(mesh):
    both = ("ctx", "exp")
    in_specs = (
        P("ctx", "exp"),
        P("ctx", None),
        P("ctx", None),
        P("ctx", "exp"),
        P(both, None),
        P(both, None),
        P(both, None),
        P(both, None),
        P(both, None),
        P("exp", None, None),
    )
    out_specs = (
        P("ctx", "exp"),
        P(both, None),
        P(both, None),
        P(both, None),
        P(both, None),
        P(both, None),
    )
    return jax.shard_map(shards, mesh=mesh, in_specs=in_specs, out_specs=out_specs, check_vma=False)
```
